32 devices in a mesh: dp: 8 (over y, x, core), cp: 4 (over z).
Axes of the slice: x: 2, y: 2, z: 4, core: 2. Of those that a mesh axis runs over, the one named last changes fastest.
Arguments:
- tokens: bfloat16 [8, 1024, 1536], P('dp', 'cp'), may hold values from -6 to 6
- routes: int32 [8, 1024, 4], P('dp', 'cp'), may hold values from 0 to 7, all different within a row; in each aligned block of 256 rows (0 to 255, 256 to 511, ..., all dimensions but the last counted through in order) at most 170 rows name the same one
- out_grad: bfloat16 [8, 1024, 1536], P('dp', 'cp'), may hold values from -6 to 6
- norm_attn: bfloat16 [1536], P('cp'), may hold values from 0.5 to 1.5
- w_query: bfloat16 [1536, 1536], P('cp'), may hold values from -0.15625 to 0.15625
- key_weight: bfloat16 [1536, 256], P('cp'), may hold values from -0.15625 to 0.15625
- value_weight: bfloat16 [1536, 256], P('cp'), may hold values from -0.15625 to 0.15625
- w_out: bfloat16 [1536, 1536], P('cp'), may hold values from -6 to 6
- norm_mix: bfloat16 [1536], P('cp'), may hold values from 0.5 to 1.5
- w_router: bfloat16 [1536, 8], P('cp'), may hold values from -0.078125 to 0.078125
- w_gate: bfloat16 [8, 1536, 768], P(None, 'cp'), may hold values from -0.15625 to 0.15625
- w_up: bfloat16 [8, 1536, 768], P(None, 'cp'), may hold values from -0.15625 to 0.15625
- w_down: bfloat16 [8, 768, 1536], P(None, 'cp'), may hold values from -0.4375 to 0.4375
Outputs:
- output: bfloat16 [8, 1024, 1536], P('dp', 'cp')
- input_grad: bfloat16 [8, 1024, 1536], P('dp', 'cp')
- grad_norm_attn: float32 [1536], P('cp')
- grad_w_query: float32 [1536, 1536], P('cp')
- grad_w_key: float32 [1536, 256], P('cp')
- grad_w_value: float32 [1536, 256], P('cp')
- grad_w_out: float32 [1536, 1536], P('cp')
- grad_norm_mix: float32 [1536], P('cp')
- grad_w_router: float32 [1536, 8], P('cp')
- grad_w_gate: float32 [8, 1536, 768], P(None, 'cp')
- grad_w_up: float32 [8, 1536, 768], P(None, 'cp')
- grad_w_down: float32 [8, 768, 1536], P(None, 'cp')
The draws below stay inside these ranges and needn't reach their ends.
Inputs may be any that keep to these rules, and one draw needn't show every extreme that they name: `routes`: each row names 4 different experts; in the rows of one device (aligned blocks of 256 rows) no expert is named by more than 170 rows.
All inputs are finite; a program needn't handle non-finite values.
Results may differ from the reference program's by a relative error of at most 0.028.
Values may be sent and summed in bfloat16 or wider, within the bound.
No kernel may reach another device: no remote copies, remote signals or barrier semaphores. Data moves between devices by JAX's collectives and lax.ppermute only.
A program may use at most 384 MiB of HBM per device.

```python
import math
import jax
import jax.numpy as jnp
import numpy as np
from jax import lax

MODEL_WIDTH = 1536
QUERY_HEADS = 12
KEY_VALUE_HEADS = 2
HEAD_WIDTH = 128
FF = 768
EXPERTS = 8
TOPK = 4
BLK = 256
TOK_DEV = 256
LEN = 1024
SEQS = 8
CAP = 170


def steps_of(rng, dims, shards, smallest, high):
    def one(dim, shards_of):
        heights = jax.random.uniform(jax.random.fold_in(jax.random.fold_in(rng, 6), dim), (shards_of,), jnp.float32, smallest / len(shards), high / len(shards))
        return jnp.repeat(jnp.exp(heights), dims[dim] // shards_of).reshape((-1,) + (1,) * (len(dims) - dim - 1))

    gain = one(*shards[0])
    for cut in shards[1:]:
        gain = gain * one(*cut)
    return gain


def routed_block(own_key, own, number, rows, amount, top, most, lean):
    ranking = jax.random.permutation(own_key, amount)
    packed, common = portions_of(amount, rows * top, most, lean, True), portions_of(amount, rows * top, most, lean, False)
    places = jnp.arange(amount)

    def named(tallies, offset_by):
        used = int((tallies > 0).sum())
        fixed = max(1, used // 4)
        shifted = fixed + (places - fixed + offset_by * (used - fixed)) % max(1, amount - fixed)
        return jnp.zeros((amount,), jnp.int32).at[ranking[jnp.where(places < fixed, places, shifted)]].set(jnp.asarray(tallies, jnp.int32))

    tallies = jnp.where(number % 4 == 0, named(packed, number // 4), named(common, number - number // 4 - 1))
    mixed = jax.random.permutation(jax.random.fold_in(own, 3), amount)
    giver, receiver = mixed[0:amount // 2 * 2:2], mixed[1:amount // 2 * 2:2]
    slack = jnp.minimum(tallies[giver] - 1, most - tallies[receiver]) // 2
    slack = jnp.where((giver == ranking[0]) | (receiver == ranking[0]) | (tallies[receiver] == 0), 0, jnp.maximum(slack, 0))
    shifted = jax.random.randint(jax.random.fold_in(own, 4), (amount // 2,), 0, 1 << 20) % (slack + 1)
    tallies = tallies.at[giver].add(-shifted).at[receiver].add(shifted)
    labels = jnp.searchsorted(jnp.cumsum(tallies), jnp.arange(rows * top), side="right").astype(jnp.int32)
    listing = labels.reshape(top, rows).T
    listing = listing[jax.random.permutation(jax.random.fold_in(own, 1), rows)]
    offset_by = jax.random.randint(jax.random.fold_in(own, 2), (rows, 1), 0, top)
    return jnp.take_along_axis(listing, (jnp.arange(top)[None, :] + offset_by) % top, axis=1)


def portions_of(amount, total, limit, lean, full):
    weights = [(1 << 20) // math.isqrt(rank ** lean) + 1 for rank in range(1, amount + 1)]
    largest = limit if full else min(limit, max(-(-total // amount), total * weights[0] // sum(weights)))
    least = 1 if total - largest >= amount - 1 else 0
    given, rest = [largest] + [least] * (amount - 1), total - largest - least * (amount - 1)
    while rest > 0:
        candidates = [i for i in range(1, amount) if given[i] < largest] or [i for i in range(1, amount) if given[i] < limit]
        pool, budget = sum([weights[i] for i in candidates]), rest
        for i in candidates:
            extra = min(limit - given[i], max(1, budget * weights[i] // pool), rest)
            given[i] = given[i] + extra
            rest = rest - extra
    return np.array(given)


def noise(key, dims, width, most, cuts=(), held_as=jnp.bfloat16):
    array = width * jax.random.normal(key, dims, jnp.float32)
    if cuts:
        array = array * steps_of(key, dims, cuts, -0.22, 0.18)
    return jnp.clip(array, -most, most).astype(held_as)


def setup_inputs(seed: int = 0) -> dict:
    key_of = jax.random.split(jax.random.key(seed), 14)
    tokens = noise(key_of[0], (SEQS, LEN, MODEL_WIDTH), 1.0, 6.0, ((0, 8), (1, 4)))
    routes_keys = jax.random.split(jax.random.fold_in(key_of[1], 1), SEQS * LEN // TOK_DEV)
    routes_turns = jax.random.permutation(jax.random.fold_in(key_of[1], 3), SEQS * LEN // TOK_DEV)
    routes = jax.vmap(lambda own, number: routed_block(jax.random.fold_in(key_of[1], 2), own, number, TOK_DEV, EXPERTS, TOPK, CAP, 1))(routes_keys, routes_turns).reshape((SEQS, LEN, TOPK))
    out_grad = noise(key_of[2], (SEQS, LEN, MODEL_WIDTH), 1.0, 6.0, ((0, 8), (1, 4)))
    norm_attn = jnp.clip(1.0 + 0.1 * jax.random.normal(key_of[3], (MODEL_WIDTH,), jnp.float32), 0.5, 1.5).astype(jnp.bfloat16)
    w_query = noise(key_of[4], (MODEL_WIDTH, QUERY_HEADS * HEAD_WIDTH), MODEL_WIDTH ** -0.5, 0.15625, ((0, 4),))
    key_weight = noise(key_of[5], (MODEL_WIDTH, KEY_VALUE_HEADS * HEAD_WIDTH), MODEL_WIDTH ** -0.5, 0.15625, ((0, 4),))
    value_weight = noise(key_of[6], (MODEL_WIDTH, KEY_VALUE_HEADS * HEAD_WIDTH), MODEL_WIDTH ** -0.5, 0.15625, ((0, 4),))
    w_out = noise(key_of[7], (QUERY_HEADS * HEAD_WIDTH, MODEL_WIDTH), (max(1, QUERY_HEADS * HEAD_WIDTH // LEN)) ** -0.5, 6.0, ((0, 4),))
    norm_mix = jnp.clip(1.0 + 0.1 * jax.random.normal(key_of[8], (MODEL_WIDTH,), jnp.float32), 0.5, 1.5).astype(jnp.bfloat16)
    w_router = noise(key_of[9], (MODEL_WIDTH, EXPERTS), (4 * MODEL_WIDTH) ** -0.5, 0.078125, ((0, 4),))
    w_gate = noise(key_of[10], (EXPERTS, MODEL_WIDTH, FF), MODEL_WIDTH ** -0.5, 0.15625, ((1, 4),))
    w_up = noise(key_of[11], (EXPERTS, MODEL_WIDTH, FF), MODEL_WIDTH ** -0.5, 0.15625, ((1, 4),))
    w_down = noise(key_of[12], (EXPERTS, FF, MODEL_WIDTH), (FF // 4) ** -0.5, 0.4375, ((1, 4),))
    return dict(tokens=tokens, routes=routes, out_grad=out_grad, norm_attn=norm_attn, w_query=w_query, key_weight=key_weight, value_weight=value_weight, w_out=w_out, norm_mix=norm_mix, w_router=w_router, w_gate=w_gate, w_up=w_up, w_down=w_down)


norm_eps = 1e-06
rope_base = 1000000.0
mask_fill = -1e+30
highest = lax.Precision.HIGHEST

@jax.custom_vjp
def lowered_input(v):
    return lax.optimization_barrier(v.astype(jnp.bfloat16)).astype(jnp.float32)

@jax.custom_vjp
def lowered_input_back(v):
    return v

def low_keep(v):
    return (lowered_input(v), None)

def low_pass(kept, grad):
    return (grad,)

def back_keep(v):
    return (v, None)

def back_low(kept, grad):
    return (lowered_input(grad),)
lowered_input.defvjp(low_keep, low_pass)
lowered_input_back.defvjp(back_keep, back_low)

def matrix_product(left, right):
    return jnp.dot(left, right, precision=highest, preferred_element_type=jnp.float32)

def norm_apply(values, gain_vec):
    inverse = lax.rsqrt(lax.optimization_barrier(jnp.mean(values * values, -1, keepdims=True)) + norm_eps)
    return values * inverse * gain_vec

def apply_rotary_embedding(values, token_positions):
    head_size = values.shape[-1]
    half_size = head_size // 2
    frequency = rope_base ** (-2.0 * jnp.arange(half_size, dtype=jnp.float32) / head_size)
    angles = token_positions.astype(jnp.float32)[:, None] * frequency[None, :]
    cosine_table = jnp.concatenate([jnp.cos(angles), jnp.cos(angles)], 1)[:, None, :]
    sine_table = jnp.concatenate([jnp.sin(angles), jnp.sin(angles)], 1)[:, None, :]
    turned = jnp.concatenate([-values[..., half_size:], values[..., :half_size]], -1)
    return values * cosine_table + turned * sine_table

def sequence_layer(seq_tokens, seq_routes, all_params):
    norm_attn, w_query, key_weight, value_weight, w_out, norm_mix, w_router, w_gate, w_up, w_down = all_params
    sequence_length = seq_tokens.shape[0]
    token_positions = jnp.arange(sequence_length, dtype=jnp.int32)
    first_normalized = lowered_input(norm_apply(seq_tokens, norm_attn))
    query_linear = lowered_input_back(matrix_product(first_normalized, w_query))
    key_linear = lowered_input_back(matrix_product(first_normalized, key_weight))
    value_entries = lowered_input(lowered_input_back(matrix_product(first_normalized, value_weight))).reshape(sequence_length, KEY_VALUE_HEADS, HEAD_WIDTH)
    rotated_query = lowered_input(apply_rotary_embedding(query_linear.reshape(sequence_length, QUERY_HEADS, HEAD_WIDTH), token_positions)).reshape(sequence_length, KEY_VALUE_HEADS, QUERY_HEADS // KEY_VALUE_HEADS, HEAD_WIDTH)
    rotated_key = lowered_input(apply_rotary_embedding(key_linear.reshape(sequence_length, KEY_VALUE_HEADS, HEAD_WIDTH), token_positions))
    scores = jnp.einsum('tgjh,sgh->gjts', rotated_query, rotated_key, precision=highest) * (1.0 / math.sqrt(HEAD_WIDTH))
    scores = lowered_input_back(scores)
    blocks = token_positions // BLK
    visible = blocks[None, :] <= blocks[:, None]
    scores = jnp.where(visible, scores, mask_fill)
    top_score = lax.optimization_barrier(jnp.max(scores, -1, keepdims=True))
    raised = jnp.exp(scores - top_score)
    prob_vals = lowered_input(raised / lax.optimization_barrier(jnp.sum(raised, -1, keepdims=True)))
    attn_mix = jnp.einsum('gjts,sgh->tgjh', prob_vals, value_entries, precision=highest).reshape(sequence_length, QUERY_HEADS * HEAD_WIDTH)
    attn_low = lowered_input(lowered_input_back(attn_mix))
    middle = seq_tokens + lowered_input_back(matrix_product(attn_low, w_out))
    normed_two = lowered_input(norm_apply(middle, norm_mix))
    logits = lowered_input_back(matrix_product(normed_two, w_router))
    chosen = jnp.take_along_axis(logits, seq_routes, 1)
    top_logit = lax.optimization_barrier(jnp.max(chosen, -1, keepdims=True))
    gate_raise = jnp.exp(chosen - top_logit)
    gate_vals = gate_raise / lax.optimization_barrier(jnp.sum(gate_raise, -1, keepdims=True))
    route_flags = (seq_routes[:, :, None] == jnp.arange(EXPERTS, dtype=jnp.int32)[None, None, :]).astype(jnp.float32)
    dense_gates = lax.optimization_barrier(jnp.sum(gate_vals[:, :, None] * route_flags, 1))
    mixture = jnp.zeros_like(middle)
    for expert in range(EXPERTS):
        gate_pre = lowered_input_back(matrix_product(normed_two, w_gate[expert]))
        up_pre = lowered_input_back(matrix_product(normed_two, w_up[expert]))
        active = lowered_input(gate_pre * jax.nn.sigmoid(gate_pre) * up_pre)
        expert_out = lowered_input_back(matrix_product(active, w_down[expert]))
        mixture = mixture + dense_gates[:, expert:expert + 1] * expert_out
    return middle + mixture

def reference(tokens, routes, out_grad, norm_attn, w_query, key_weight, value_weight, w_out, norm_mix, w_router, w_gate, w_up, w_down):
    params = tuple((weight_arr.astype(jnp.float32) for weight_arr in (norm_attn, w_query, key_weight, value_weight, w_out, norm_mix, w_router, w_gate, w_up, w_down)))
    start_tokens = tokens.astype(jnp.float32)

    def forward(all_tokens, all_params):

        def one_sequence(seq_pair):
            return sequence_layer(seq_pair[0], seq_pair[1], all_params)
        return lax.map(jax.checkpoint(one_sequence), (all_tokens, routes))
    result, pullback = jax.vjp(forward, start_tokens, params)
    token_grad, param_grads = pullback(out_grad.astype(jnp.float32))
    return (result.astype(jnp.bfloat16), token_grad.astype(jnp.bfloat16), param_grads[0], param_grads[1], param_grads[2], param_grads[3], param_grads[4], param_grads[5], param_grads[6], param_grads[7], param_grads[8], param_grads[9])
```

```python
import functools
import math

import jax
import jax.numpy as jnp
from jax import lax
from jax.experimental import pallas as pl
from jax.experimental.pallas import tpu as pltpu
from jax.sharding import PartitionSpec as P

MODEL_WIDTH = 1536
QUERY_HEADS = 12
KEY_VALUE_HEADS = 2
HEAD_WIDTH = 128
EXPERTS = 8
TOPK = 4
BLK = 256

norm_eps = 1e-06
rope_base = 1000000.0
mask_fill = -1e30
score_scale = 1.0 / math.sqrt(HEAD_WIDTH)
query_columns = QUERY_HEADS * HEAD_WIDTH
key_columns = KEY_VALUE_HEADS * HEAD_WIDTH
group_heads = QUERY_HEADS // KEY_VALUE_HEADS

f32 = jnp.float32
bf16 = jnp.bfloat16


def dot_nn(a, b):
    return lax.dot_general(a, b, (((1,), (0,)), ((), ())), preferred_element_type=f32)


def dot_nt(a, b):
    return lax.dot_general(a, b, (((1,), (1,)), ((), ())), preferred_element_type=f32)


def dot_tn(a, b):
    return lax.dot_general(a, b, (((0,), (0,)), ((), ())), preferred_element_type=f32)


def params(megabytes):
    return pltpu.CompilerParams(vmem_limit_bytes=megabytes * 1024 * 1024)


def project_kernel(chunk_heads, slot_ref, h_ref, w_ref, cos_ref, sin_ref, out_ref):
    j = pl.program_id(0)
    full = dot_nn(h_ref[...], w_ref[0])
    for k in range(chunk_heads):
        u = full[:, k * HEAD_WIDTH : (k + 1) * HEAD_WIDTH]
        turned = u * cos_ref[...] + pltpu.roll(u, HEAD_WIDTH // 2, 1) * sin_ref[...]
        is_value = j * chunk_heads + k >= QUERY_HEADS + KEY_VALUE_HEADS
        out_ref[:, k * HEAD_WIDTH : (k + 1) * HEAD_WIDTH] = jnp.where(is_value, u, turned).astype(bf16)


def project(slot_of, h, w_rel, cos, sin):
    m, d, cw = w_rel.shape
    t = h.shape[0]
    return pl.pallas_call(
        functools.partial(project_kernel, cw // HEAD_WIDTH),
        grid_spec=pltpu.PrefetchScalarGridSpec(
            num_scalar_prefetch=1,
            grid=(m,),
            in_specs=[
                pl.BlockSpec((t, d), lambda j, s: (0, 0)),
                pl.BlockSpec((1, d, cw), lambda j, s: (s[j], 0, 0)),
                pl.BlockSpec((t, HEAD_WIDTH), lambda j, s: (0, 0)),
                pl.BlockSpec((t, HEAD_WIDTH), lambda j, s: (0, 0)),
            ],
            out_specs=pl.BlockSpec((t, cw), lambda j, s: (0, j)),
        ),
        out_shape=jax.ShapeDtypeStruct((t, m * cw), bf16),
        compiler_params=params(24),
        cost_estimate=pl.CostEstimate(
            flops=2 * t * d * m * cw, bytes_accessed=2 * d * m * cw, transcendentals=0
        ),
        name="project",
    )(slot_of, h, w_rel, cos, sin)


def project_back_kernel(chunk_ref, h_ref, g_ref, w_ref, dh_ref, gw_ref):
    @pl.when(pl.program_id(0) == 0)
    def _():
        dh_ref[...] = jnp.zeros_like(dh_ref)

    dh_ref[...] += dot_nt(g_ref[...], w_ref[0])
    gw_ref[0] = dot_tn(h_ref[...], g_ref[...]).astype(bf16)


def project_back(chunk_of, h, grad, w_rel):
    m, d, cw = w_rel.shape
    t = h.shape[0]
    return pl.pallas_call(
        project_back_kernel,
        grid_spec=pltpu.PrefetchScalarGridSpec(
            num_scalar_prefetch=1,
            grid=(m,),
            in_specs=[
                pl.BlockSpec((t, d), lambda j, c: (0, 0)),
                pl.BlockSpec((t, cw), lambda j, c: (0, c[j])),
                pl.BlockSpec((1, d, cw), lambda j, c: (j, 0, 0)),
            ],
            out_specs=[
                pl.BlockSpec((t, d), lambda j, c: (0, 0)),
                pl.BlockSpec((1, d, cw), lambda j, c: (j, 0, 0)),
            ],
        ),
        out_shape=[
            jax.ShapeDtypeStruct((t, d), f32),
            jax.ShapeDtypeStruct((m, d, cw), bf16),
        ],
        compiler_params=params(32),
        cost_estimate=pl.CostEstimate(
            flops=4 * t * d * m * cw, bytes_accessed=4 * d * m * cw, transcendentals=0
        ),
        name="project_back",
    )(chunk_of, h, grad, w_rel)


def attend_kernel(seen_ref, q_ref, k_ref, v_ref, out_ref):
    s = dot_nt(q_ref[...], k_ref[...]) * score_scale
    col = lax.broadcasted_iota(jnp.int32, s.shape, 1)
    s = jnp.where(col < seen_ref[0], s, mask_fill)
    e = jnp.exp(s - jnp.max(s, 1, keepdims=True))
    p = (e / jnp.sum(e, 1, keepdims=True)).astype(bf16)
    out_ref[...] = dot_nn(p, v_ref[...]).astype(bf16)


def attend(seen, qkv, kv):
    t, rows = qkv.shape[0], kv.shape[0]
    return pl.pallas_call(
        attend_kernel,
        grid_spec=pltpu.PrefetchScalarGridSpec(
            num_scalar_prefetch=1,
            grid=(QUERY_HEADS,),
            in_specs=[
                pl.BlockSpec((t, HEAD_WIDTH), lambda j, s: (0, j)),
                pl.BlockSpec((rows, HEAD_WIDTH), lambda j, s: (0, j // group_heads)),
                pl.BlockSpec((rows, HEAD_WIDTH), lambda j, s: (0, KEY_VALUE_HEADS + j // group_heads)),
            ],
            out_specs=pl.BlockSpec((t, HEAD_WIDTH), lambda j, s: (0, j)),
        ),
        out_shape=jax.ShapeDtypeStruct((t, query_columns), bf16),
        compiler_params=params(40),
        cost_estimate=pl.CostEstimate(
            flops=4 * t * rows * query_columns,
            bytes_accessed=4 * t * query_columns,
            transcendentals=t * rows * QUERY_HEADS,
        ),
        name="attend",
    )(seen, qkv, kv, kv)


def attend_back_kernel(seen_ref, q_ref, k_ref, v_ref, g_ref, cos_ref, sin_ref, dq_ref, dkv_ref, dk_acc, dv_acc):
    j = pl.program_id(0)
    q, k, g = q_ref[...], k_ref[...], g_ref[...]
    s = dot_nt(k, q) * score_scale
    row = lax.broadcasted_iota(jnp.int32, s.shape, 0)
    s = jnp.where(row < seen_ref[0], s, mask_fill)
    e = jnp.exp(s - jnp.max(s, 0, keepdims=True))
    p = e / jnp.sum(e, 0, keepdims=True)
    pb = p.astype(bf16)
    dp = dot_nt(v_ref[...], g)
    delta = jnp.sum(p * dp, 0, keepdims=True)
    ds = (p * (dp - delta)).astype(bf16)
    dq = dot_tn(ds, k) * score_scale
    dq_ref[...] = (dq * cos_ref[...] - pltpu.roll(dq, HEAD_WIDTH // 2, 1) * sin_ref[...]).astype(bf16)

    @pl.when(j % group_heads == 0)
    def _():
        dk_acc[...] = jnp.zeros_like(dk_acc)
        dv_acc[...] = jnp.zeros_like(dv_acc)

    dk_acc[...] += dot_nn(ds, q) * score_scale
    dv_acc[...] += dot_nn(pb, g)

    @pl.when(j % group_heads == group_heads - 1)
    def _():
        dkv_ref[0] = dk_acc[...].astype(bf16)
        dkv_ref[1] = dv_acc[...].astype(bf16)


def attend_back(seen, qkv, kv, grad, cos, sin):
    t, rows = qkv.shape[0], kv.shape[0]
    return pl.pallas_call(
        attend_back_kernel,
        grid_spec=pltpu.PrefetchScalarGridSpec(
            num_scalar_prefetch=1,
            grid=(QUERY_HEADS,),
            in_specs=[
                pl.BlockSpec((t, HEAD_WIDTH), lambda j, s: (0, j)),
                pl.BlockSpec((rows, HEAD_WIDTH), lambda j, s: (0, j // group_heads)),
                pl.BlockSpec((rows, HEAD_WIDTH), lambda j, s: (0, KEY_VALUE_HEADS + j // group_heads)),
                pl.BlockSpec((t, HEAD_WIDTH), lambda j, s: (0, j)),
                pl.BlockSpec((t, HEAD_WIDTH), lambda j, s: (0, 0)),
                pl.BlockSpec((t, HEAD_WIDTH), lambda j, s: (0, 0)),
            ],
            out_specs=[
                pl.BlockSpec((t, HEAD_WIDTH), lambda j, s: (0, j)),
                pl.BlockSpec((2, rows, HEAD_WIDTH), lambda j, s: (0, 0, j // group_heads)),
            ],
            scratch_shapes=[pltpu.VMEM((rows, HEAD_WIDTH), f32)] * 2,
        ),
        out_shape=[
            jax.ShapeDtypeStruct((t, query_columns), bf16),
            jax.ShapeDtypeStruct((2, rows, key_columns), bf16),
        ],
        compiler_params=params(56),
        cost_estimate=pl.CostEstimate(
            flops=10 * t * rows * query_columns,
            bytes_accessed=8 * t * query_columns,
            transcendentals=t * rows * QUERY_HEADS,
        ),
        name="attend_back",
    )(seen, qkv, kv, kv, grad, cos, sin)


def experts_kernel(
    fc, h_ref, z_ref, gate_ref, wg_ref, wu_ref, wd_ref,
    a_ref, dg_ref, du_ref, eo_ref, dh_ref, dgate_ref, eo_acc, dh_acc, dgate_acc,
):
    step = pl.program_id(0)
    ct = a_ref.shape[1]
    wg = wg_ref[...].reshape(ct, wg_ref.shape[-1])
    wu = wu_ref[...].reshape(ct, wu_ref.shape[-1])
    wd = wd_ref[...].reshape(ct, wd_ref.shape[-1])
    slot_row = lax.broadcasted_iota(jnp.int32, (gate_ref.shape[0], ct), 0)
    slot_col = lax.broadcasted_iota(jnp.int32, (gate_ref.shape[0], ct), 1) + step * ct
    low = slot_row * fc
    pick = jnp.where((slot_col >= low) & (slot_col < low + fc), 1.0, 0.0).astype(bf16)
    gates = gate_ref[...]
    gates_high = gates.astype(bf16)
    gates_low = (gates - gates_high.astype(f32)).astype(bf16)
    wide = dot_tn(gates_high, pick) + dot_tn(gates_low, pick)
    g = dot_nt(h_ref[...], wg)
    u = dot_nt(h_ref[...], wu)
    e = dot_nt(z_ref[...], wd)
    sig = 1.0 / (1.0 + jnp.exp(-g))
    swish = g * sig
    a = swish * u
    da = e * wide
    ab = (a * wide).astype(bf16)
    dg = (da * u * (sig * (1.0 + g * (1.0 - sig)))).astype(bf16)
    du = (da * swish).astype(bf16)
    a_ref[...] = ab
    dg_ref[...] = dg
    du_ref[...] = du

    @pl.when(step == 0)
    def _():
        eo_acc[...] = jnp.zeros_like(eo_acc)
        dh_acc[...] = jnp.zeros_like(dh_acc)
        dgate_acc[...] = jnp.zeros_like(dgate_acc)

    dgate_acc[...] += dot_nt(pick, (a * e).astype(bf16))
    eo_acc[...] += dot_nn(ab, wd)
    dh_acc[...] += dot_nn(dg, wg) + dot_nn(du, wu)

    @pl.when(step == pl.num_programs(0) - 1)
    def _():
        eo_ref[...] = eo_acc[...].astype(eo_ref.dtype)
        dh_ref[...] = dh_acc[...].astype(dh_ref.dtype)
        dgate_ref[...] = dgate_acc[...]


def experts(h, z, gates, wg, wu, wd, sent_type):
    t, d = h.shape
    m, fc = wg.shape[0], wg.shape[1]
    width = m * fc
    ct = min(width, 384)
    per = ct // fc
    w_spec = pl.BlockSpec((per, fc, d), lambda j: (j, 0, 0))
    rows = pl.BlockSpec((t, d), lambda j: (0, 0))
    tile = pl.BlockSpec((t, ct), lambda j: (0, j))
    slots = pl.BlockSpec(gates.shape, lambda j: (0, 0))
    return pl.pallas_call(
        functools.partial(experts_kernel, fc),
        grid=(width // ct,),
        in_specs=[rows, rows, slots, w_spec, w_spec, w_spec],
        out_specs=[tile, tile, tile, rows, rows, slots],
        out_shape=[
            jax.ShapeDtypeStruct((t, width), bf16),
            jax.ShapeDtypeStruct((t, width), bf16),
            jax.ShapeDtypeStruct((t, width), bf16),
            jax.ShapeDtypeStruct((t, d), sent_type),
            jax.ShapeDtypeStruct((t, d), sent_type),
            jax.ShapeDtypeStruct(gates.shape, f32),
        ],
        scratch_shapes=[
            pltpu.VMEM((t, d), f32),
            pltpu.VMEM((t, d), f32),
            pltpu.VMEM(gates.shape, f32),
        ],
        compiler_params=params(44),
        cost_estimate=pl.CostEstimate(
            flops=12 * t * d * width, bytes_accessed=6 * d * width, transcendentals=t * width
        ),
        name="experts",
    )(h, z, gates, wg, wu, wd)


def expert_grads_kernel(n, fc, *refs):
    a, dg, du = refs[:n], refs[n : 2 * n], refs[2 * n : 3 * n]
    h, z, out_ref = refs[3 * n : 4 * n], refs[4 * n : 5 * n], refs[5 * n]
    per = out_ref.shape[0]
    for which, (left, right) in enumerate(((dg, h), (du, h), (a, z))):
        total = dot_tn(left[0][...], right[0][...])
        for s in range(1, n):
            total += dot_tn(left[s][...], right[s][...])
        out_ref[:, which] = total.astype(bf16).reshape(per, fc, total.shape[-1])


def expert_grads(fc, a, dg, du, h, z):
    n = len(a)
    t, width = a[0].shape
    d = h[0].shape[1]
    ct = min(width, 384)
    per = ct // fc
    tile = pl.BlockSpec((t, ct), lambda j: (0, j))
    rows = pl.BlockSpec((t, d), lambda j: (0, 0))
    return pl.pallas_call(
        functools.partial(expert_grads_kernel, n, fc),
        grid=(width // ct,),
        in_specs=[tile] * (3 * n) + [rows] * (2 * n),
        out_specs=pl.BlockSpec((per, 3, fc, d), lambda j: (j, 0, 0, 0)),
        out_shape=jax.ShapeDtypeStruct((width // fc, 3, fc, d), bf16),
        compiler_params=params(58),
        cost_estimate=pl.CostEstimate(
            flops=6 * n * t * d * width, bytes_accessed=6 * d * width, transcendentals=0
        ),
        name="expert_grads",
    )(*a, *dg, *du, *h, *z)


def pick_kernel(where_ref, in_ref, out_ref):
    out_ref[...] = in_ref[...].reshape(out_ref.shape).astype(out_ref.dtype)


def reorder(where, stacked):
    m = stacked.shape[0]
    block = (1,) + stacked.shape[1:]
    tail = (0,) * (stacked.ndim - 1)
    return pl.pallas_call(
        pick_kernel,
        grid_spec=pltpu.PrefetchScalarGridSpec(
            num_scalar_prefetch=1,
            grid=(m,),
            in_specs=[pl.BlockSpec(block, lambda j, w: (w[j],) + tail)],
            out_specs=pl.BlockSpec(block, lambda j, w: (j,) + tail),
        ),
        out_shape=jax.ShapeDtypeStruct(stacked.shape, stacked.dtype),
        compiler_params=params(16),
        cost_estimate=pl.CostEstimate(flops=0, bytes_accessed=4 * stacked.size, transcendentals=0),
        name="reorder",
    )(where, stacked)


def reorder_rows(where, stacked, inner_first):
    m, n, c, d = stacked.shape if inner_first else (stacked.shape[1], stacked.shape[0]) + stacked.shape[2:]
    one, two = (1, n, c, d), (n, 1, c, d)
    pick_m, put_m = (lambda j, w: (w[j], 0, 0, 0)), (lambda j, w: (j, 0, 0, 0))
    pick_n, put_n = (lambda j, w: (0, w[j], 0, 0)), (lambda j, w: (0, j, 0, 0))
    return pl.pallas_call(
        pick_kernel,
        grid_spec=pltpu.PrefetchScalarGridSpec(
            num_scalar_prefetch=1,
            grid=(m,),
            in_specs=[pl.BlockSpec(one, pick_m) if inner_first else pl.BlockSpec(two, pick_n)],
            out_specs=pl.BlockSpec(two, put_n) if inner_first else pl.BlockSpec(one, put_m),
        ),
        out_shape=jax.ShapeDtypeStruct((n, m, c, d) if inner_first else (m, n, c, d), stacked.dtype),
        compiler_params=params(16),
        cost_estimate=pl.CostEstimate(flops=0, bytes_accessed=4 * stacked.size, transcendentals=0),
        name="reorder_rows",
    )(where, stacked)


def spread_kernel(half, slot_ref, near_ref, far_ref, out_ref):
    near = slot_ref[pl.program_id(0)] < half

    @pl.when(near)
    def _():
        out_ref[...] = near_ref[...].astype(f32)

    @pl.when(jnp.logical_not(near))
    def _():
        out_ref[...] = far_ref[...].astype(f32)


def spread(slot_of, near, far):
    half = near.shape[0]
    block = (1,) + near.shape[1:]
    tail = (0,) * (near.ndim - 1)
    return pl.pallas_call(
        functools.partial(spread_kernel, half),
        grid_spec=pltpu.PrefetchScalarGridSpec(
            num_scalar_prefetch=1,
            grid=(2 * half,),
            in_specs=[
                pl.BlockSpec(block, lambda j, s: (jnp.minimum(s[j], half - 1),) + tail),
                pl.BlockSpec(block, lambda j, s: (jnp.maximum(s[j] - half, 0),) + tail),
            ],
            out_specs=pl.BlockSpec(block, lambda j, s: (j,) + tail),
        ),
        out_shape=jax.ShapeDtypeStruct((2 * half,) + near.shape[1:], f32),
        compiler_params=params(16),
        cost_estimate=pl.CostEstimate(flops=0, bytes_accessed=12 * near.size, transcendentals=0),
        name="spread",
    )(slot_of, near, far)


class Along:
    def __init__(self):
        self.n, self.m = lax.axis_size("cp"), lax.axis_size("dp")
        self.r, self.i = lax.axis_index("cp"), lax.axis_index("dp")
        self.bits = self.m.bit_length() - 1
        assert 1 << self.bits == self.m and self.bits > 1
        self.inner = self.bits - 1
        slots = jnp.arange(self.m, dtype=jnp.int32)
        self.chunk_of = self.i ^ (((slots & (self.m // 2 - 1)) << 1) | (slots >> self.inner))
        offset = slots ^ self.i
        self.slot_of = (offset >> 1) | ((offset & 1) << self.inner)

    def swap(self, x, bit):
        mask = 1 if bit == self.inner else 2 << bit
        return lax.ppermute(x, "dp", [(k, k ^ mask) for k in range(self.m)])

    def shift(self, x, s):
        return lax.ppermute(x, "cp", [(k, (k + s) % self.n) for k in range(self.n)])

    def shift_up(self, x, s):
        return lax.ppermute(x, "cp", [(k, k + s) for k in range(self.n - s)])

    def shift_down(self, x, s):
        return lax.ppermute(x, "cp", [(k + s, k) for k in range(self.n - s)])

    def orders(self):
        up = list(range(self.inner))
        return up, up[::-1]

    def gather_dp(self, x, order):
        buffer, held = x[None], [0]
        for bit in order:
            got = self.swap(buffer, bit)
            buffer = jnp.concatenate([buffer, got], 0)
            held = held + [h | 1 << bit for h in held]
        if held != sorted(held):
            buffer = jnp.concatenate([buffer[held.index(h)][None] for h in sorted(held)], 0)
        return buffer, self.swap(buffer, self.inner)

    def halve_core(self, x):
        half = self.m // 2
        return (x[:half].astype(f32) + self.swap(x[half:], self.inner).astype(f32)).astype(bf16)

    def halve(self, x, order):
        held = list(range(self.m // 2))
        parts = {h: x[h] for h in held}
        for bit in order:
            sent = [h for h in held if h >> bit & 1]
            held = [h for h in held if not h >> bit & 1]
            got = self.swap(jnp.stack([parts[h].astype(bf16) for h in sent]), bit)
            for k, h in enumerate(held):
                parts[h] = parts[h].astype(f32) + got[k].astype(f32)
        return parts[0]

    def pieces(self, x, s):
        return lax.dynamic_index_in_dim(x, (self.r + s) % self.n, 0, keepdims=False)

    def scatter_cp(self, x):
        return [self.pieces(x, 0)] + [self.shift(self.pieces(x, s), s) for s in range(1, self.n)]

    def ranked(self, slots):
        back = slots[::-1]
        line = jnp.stack(back + back[:-1])
        return lax.dynamic_slice_in_dim(line, self.n - 1 - self.r, self.n, 0)

    def gather_cp(self, x):
        return self.ranked([x] + [self.shift(x, s) for s in range(1, self.n)])


def norm_forward(values, gain_vec):
    inverse = lax.rsqrt(jnp.mean(values * values, -1, keepdims=True) + norm_eps)
    scaled = values * inverse
    return (scaled * gain_vec, scaled, inverse)


def norm_backward(gradient, gain_vec, scaled, inverse):
    gain_grad = jnp.sum(gradient * scaled, 0)
    inner_vals = gradient * gain_vec
    return (
        inverse * (inner_vals - scaled * jnp.mean(inner_vals * scaled, -1, keepdims=True)),
        gain_grad,
    )


def rotary(positions):
    half = HEAD_WIDTH // 2
    frequency = rope_base ** (-2.0 * jnp.arange(half, dtype=f32) / HEAD_WIDTH)
    angles = positions.astype(f32)[:, None] * frequency[None, :]
    cos, sin = jnp.cos(angles), jnp.sin(angles)
    return jnp.concatenate([cos, cos], 1), jnp.concatenate([-sin, sin], 1)


def local(
    tokens, routes, out_grad, norm_attn, w_query, key_weight, value_weight, w_out,
    norm_mix, w_router, w_gate, w_up, w_down,
):
    along = Along()
    n, m, r, i = along.n, along.m, along.r, along.i
    t, d = tokens.shape[1], tokens.shape[2]
    assert t == BLK
    dl, ff, fs = w_query.shape[0], w_gate.shape[2], w_down.shape[1]
    sub = m // EXPERTS
    fc = fs // sub
    rc = dl // m
    up_order, down_order = along.orders()
    inputs = tokens[0].astype(f32)
    route_rows = routes[0]
    dz = out_grad[0]

    w_qkv = jnp.concatenate([w_query, key_weight, value_weight], 1)
    cw = w_qkv.shape[1] // m
    own_qkv = along.gather_cp(lax.dynamic_slice_in_dim(w_qkv, i * cw, cw, 1)).reshape(d, cw)
    small = jnp.concatenate([norm_attn[None], norm_mix[None], w_router.T], 0)
    small = jnp.swapaxes(along.gather_cp(small), 0, 1).reshape(2 + EXPERTS, d)
    gain_one, gain_two = small[0].astype(f32), small[1].astype(f32)
    router = small[2:]
    qkv_a = along.gather_dp(own_qkv[: d // 2], up_order)
    qkv_b = along.gather_dp(own_qkv[d // 2 :], down_order)
    w_rel = jnp.concatenate([jnp.concatenate(qkv_a, 0), jnp.concatenate(qkv_b, 0)], 1)

    normed_one, scaled_one, inverse_one = norm_forward(inputs, gain_one)
    h1 = normed_one.astype(bf16)
    cos, sin = rotary(r * t + jnp.arange(t, dtype=jnp.int32))
    qkv = project(along.slot_of, h1, w_rel, cos, sin)
    own_kv = qkv[:, query_columns:]
    kv = jnp.concatenate([own_kv] + [along.shift_up(own_kv, s) for s in range(1, n)], 0)
    seen = ((r + 1) * t).reshape(1)
    ob = attend(seen, qkv, kv)

    expert_chunk = i // sub
    flipped = [
        lax.dynamic_index_in_dim(w, expert_chunk, 0, keepdims=False).T.reshape(n, sub, fc, dl)
        for w in (w_gate, w_up)
    ]
    flipped = jnp.stack(flipped, 1)
    flipped = lax.dynamic_index_in_dim(flipped, i % sub, 2, keepdims=False)
    gate_up = along.ranked(along.scatter_cp(flipped))
    gate_up = jnp.transpose(gate_up, (1, 2, 0, 3)).reshape(2, fc, d)
    own_out = along.gather_cp(lax.dynamic_slice_in_dim(w_out, i * rc, rc, 0))
    own_out = own_out.reshape(2, n * rc // 2, d)
    mix_a = along.gather_dp(jnp.concatenate([gate_up[0], own_out[0]], 0), up_order)
    mix_b = along.gather_dp(jnp.concatenate([gate_up[1], own_out[1]], 0), down_order)
    wg = jnp.concatenate([x[:, :fc] for x in mix_a], 0)
    wu = jnp.concatenate([x[:, :fc] for x in mix_b], 0)
    out_rel = jnp.concatenate(
        [jnp.concatenate([a[:, fc:], b[:, fc:]], 1) for a, b in zip(mix_a, mix_b)], 0
    ).reshape(m, n, rc, d)
    full_out = reorder_rows(along.slot_of, out_rel, True).reshape(n * dl, d)
    wd = reorder(along.chunk_of, w_down.reshape(m, fc, d))

    middle = inputs + dot_nn(ob, full_out)
    normed_two, scaled_two, inverse_two = norm_forward(middle, gain_two)
    h2 = normed_two.astype(bf16)
    logits = dot_nt(h2, router)
    experts_range = jnp.arange(EXPERTS, dtype=jnp.int32)
    route_flags = (route_rows[:, :, None] == experts_range).astype(f32)
    chosen = jnp.sum(logits[:, None, :] * route_flags, -1)
    raised = jnp.exp(chosen - jnp.max(chosen, -1, keepdims=True))
    gate_vals = raised / jnp.sum(raised, -1, keepdims=True)
    slot_flags = (route_rows[:, :, None] == along.chunk_of // sub).astype(f32)
    gates = jnp.sum(gate_vals[:, :, None] * slot_flags, 1).T
    padded = max(m, 16)
    gates = jnp.concatenate([gates, jnp.zeros((padded - m, t), f32)], 0)

    z_slots = [dz] + [along.shift(dz, s) for s in range(1, n)]
    h_slots = [h2] + [along.shift(h2, s) for s in range(1, n)]
    gate_slots = [gates] + [along.shift(gates, s) for s in range(1, n)]
    done = [
        experts(h_slots[s], z_slots[s], gate_slots[s], wg, wu, wd, f32 if s == 0 else bf16)
        for s in range(n)
    ]
    mixed, h2_grad, slot_gate_grad = done[0][3], done[0][4], done[0][5]
    for s in range(1, n):
        h2_grad = h2_grad + along.shift(done[s][4], -s).astype(f32)
        slot_gate_grad = slot_gate_grad + along.shift(done[s][5], -s)
    for s in range(1, n):
        mixed = mixed + along.shift(done[s][3], -s).astype(f32)
    output = (middle + mixed).astype(bf16)[None]
    mix_grads = expert_grads(fc, *([x[k] for x in done] for k in range(3)), h_slots, z_slots)

    gate_grad = jnp.sum(slot_gate_grad[:m].T[:, None, :] * slot_flags, -1)
    weighted = gate_vals * gate_grad
    chosen_grad = weighted - gate_vals * jnp.sum(weighted, -1, keepdims=True)
    logit_grad = jnp.sum(chosen_grad[:, :, None] * route_flags, 1).astype(bf16)
    router_grad = dot_tn(logit_grad, h2)
    h2_grad = h2_grad + dot_nn(logit_grad, router)
    middle_norm_grad, gain_two_grad = norm_backward(h2_grad, gain_two, scaled_two, inverse_two)
    middle_grad = dz.astype(f32) + middle_norm_grad
    branch = middle_grad.astype(bf16)

    dob = dot_nt(branch, full_out).astype(bf16)
    out_grads = dot_tn(ob, branch).astype(bf16)
    out_grads = reorder_rows(along.chunk_of, out_grads.reshape(n, m, rc, d), False)
    dq, dkv = attend_back(seen, qkv, kv, dob, cos, sin)
    dkv_own = dkv[:, :t].astype(f32)
    for s in range(1, n):
        dkv_own = dkv_own + along.shift_down(dkv[:, s * t : (s + 1) * t], s).astype(f32)
    dk = dkv_own[0].reshape(t, KEY_VALUE_HEADS, HEAD_WIDTH)
    half = HEAD_WIDTH // 2
    dk = dk * cos[:, None] - jnp.concatenate([dk[..., half:], dk[..., :half]], -1) * sin[:, None]
    dqkv = jnp.concatenate([dq, dk.reshape(t, key_columns).astype(bf16), dkv_own[1].astype(bf16)], 1)
    h1_grad, qkv_grads = project_back(along.chunk_of, h1, dqkv, w_rel)
    input_norm_grad, gain_one_grad = norm_backward(h1_grad, gain_one, scaled_one, inverse_one)
    input_grad = (middle_grad + input_norm_grad).astype(bf16)[None]

    mix_grads = along.halve_core(mix_grads.reshape(m, 3 * fc, d))
    cut = 3 * fc // 2
    own_mix = jnp.concatenate(
        [along.halve(mix_grads[:, :cut], down_order), along.halve(mix_grads[:, cut:], up_order)], 0
    ).astype(bf16)
    down_half = fc // 2
    down_a = along.gather_dp(own_mix[2 * fc : 2 * fc + down_half], up_order)
    down_b = along.gather_dp(own_mix[2 * fc + down_half :], down_order)
    down_near = jnp.concatenate([down_a[0], down_b[0]], 1)
    down_far = jnp.concatenate([down_a[1], down_b[1]], 1)
    grad_w_down = spread(along.slot_of, down_near, down_far).reshape(EXPERTS, fs, d)
    back = jnp.transpose(own_mix[: 2 * fc].reshape(2 * fc, n, dl), (1, 0, 2))
    back = along.ranked(along.scatter_cp(back)).reshape(n, 2, fc, dl)
    back = jnp.transpose(back, (1, 3, 0, 2)).reshape(2, dl, n * fc)
    grads = []
    for k, order in ((0, up_order), (1, down_order)):
        near, far = along.gather_dp(back[k], order)
        g = spread(along.slot_of, near, far)
        if sub > 1:
            g = g.reshape(EXPERTS, sub, dl, n, fc)
            g = jnp.transpose(g, (0, 2, 3, 1, 4))
        grads.append(g.reshape(EXPERTS, dl, ff))
    grad_w_gate, grad_w_up = grads

    def sum_all(x):
        x = along.halve_core(x)
        cut = x.shape[1] // 2
        own = jnp.concatenate([along.halve(x[:, :cut], down_order), along.halve(x[:, cut:], up_order)], 0)
        return own.astype(bf16)

    own_out = along.scatter_cp(sum_all(out_grads.reshape(m, n * rc, d)).reshape(n, rc, d))
    own_out = functools.reduce(jnp.add, [x.astype(f32) for x in own_out]).astype(bf16)
    near, far = along.gather_dp(own_out, up_order)
    grad_w_out = spread(along.slot_of, near, far).reshape(dl, d)
    own_qkv = along.scatter_cp(sum_all(qkv_grads).reshape(n, dl, cw))
    own_qkv = functools.reduce(jnp.add, [x.astype(f32) for x in own_qkv]).astype(bf16)
    near, far = along.gather_dp(own_qkv, down_order)
    qkv_grad = jnp.transpose(spread(along.slot_of, near, far), (1, 0, 2)).reshape(dl, m * cw)
    grad_w_query = qkv_grad[:, :query_columns]
    grad_w_key = qkv_grad[:, query_columns : query_columns + key_columns]
    grad_w_value = qkv_grad[:, query_columns + key_columns :]

    small_grads = jnp.concatenate([gain_one_grad[None], gain_two_grad[None], router_grad], 0)
    small_grads = jnp.transpose(small_grads.reshape(2 + EXPERTS, n, dl), (1, 0, 2))
    small_grads = functools.reduce(jnp.add, along.scatter_cp(small_grads))
    for bit in range(along.bits):
        small_grads = small_grads + along.swap(small_grads, bit)
    return (
        output,
        input_grad,
        small_grads[0],
        grad_w_query,
        grad_w_key,
        grad_w_value,
        grad_w_out,
        small_grads[1],
        small_grads[2:].T,
        grad_w_gate,
        grad_w_up,
        grad_w_down,
    )


def solution(mesh):
    seq = P("dp", "cp", None)
    row, mid = P("cp", None), P(None, "cp", None)
    in_specs = (seq, seq, seq, P("cp"), row, row, row, row, P("cp"), row, mid, mid, mid)
    out_specs = (seq, seq, P("cp"), row, row, row, row, P("cp"), row, mid, mid, mid)
    return jax.shard_map(local, mesh=mesh, in_specs=in_specs, out_specs=out_specs, check_vma=False)
```

```python
import functools
import math

import jax
import jax.numpy as jnp
from jax import lax
from jax.experimental import pallas as pl
from jax.experimental.pallas import tpu as pltpu
from jax.sharding import PartitionSpec as P

MODEL_WIDTH = 1536
QUERY_HEADS = 12
KEY_VALUE_HEADS = 2
HEAD_WIDTH = 128
EXPERTS = 8
TOPK = 4
BLK = 256

norm_eps = 1e-06
rope_base = 1000000.0
mask_fill = -1e30
score_scale = 1.0 / math.sqrt(HEAD_WIDTH)
query_columns = QUERY_HEADS * HEAD_WIDTH
key_columns = KEY_VALUE_HEADS * HEAD_WIDTH
group_heads = QUERY_HEADS // KEY_VALUE_HEADS

COST = 100000
EXTRA = 16
f32 = jnp.float32
bf16 = jnp.bfloat16


def dot_nn(a, b):
    return lax.dot_general(a, b, (((1,), (0,)), ((), ())), preferred_element_type=f32)


def dot_nt(a, b):
    return lax.dot_general(a, b, (((1,), (1,)), ((), ())), preferred_element_type=f32)


def dot_tn(a, b):
    return lax.dot_general(a, b, (((0,), (0,)), ((), ())), preferred_element_type=f32)


def params(megabytes):
    return pltpu.CompilerParams(vmem_limit_bytes=megabytes * 1024 * 1024)


def cost(flops, moved, raised=0):
    return pl.CostEstimate(flops=flops // COST, bytes_accessed=moved // COST, transcendentals=raised // COST)


def after(x, *deps):
    return lax.optimization_barrier((x, deps))[0]


def project_kernel(chunk_heads, half, slot_ref, h_ref, an_ref, af_ref, bn_ref, bf_ref, cos_ref, sin_ref, out_ref):
    j = pl.program_id(0)
    near = slot_ref[j] < half
    cut = an_ref.shape[1]

    def run(a_ref, b_ref):
        full = dot_nn(h_ref[:, :cut], a_ref[0]) + dot_nn(h_ref[:, cut:], b_ref[0])
        for k in range(chunk_heads):
            at = slice(k * HEAD_WIDTH, (k + 1) * HEAD_WIDTH)
            u = full[:, at]
            turned = u * cos_ref[...] + pltpu.roll(u, HEAD_WIDTH // 2, 1) * sin_ref[...]
            is_value = j * chunk_heads + k >= QUERY_HEADS + KEY_VALUE_HEADS
            out_ref[:, at] = jnp.where(is_value, u, turned).astype(bf16)

    pl.when(near)(lambda: run(an_ref, bn_ref))
    pl.when(jnp.logical_not(near))(lambda: run(af_ref, bf_ref))


def project(slot_of, h, w_a, w_b, cos, sin):
    half, cut, cw = w_a[0].shape
    t, d = h.shape
    m = 2 * half
    w_spec = pl.BlockSpec((1, cut, cw), lambda j, s: (s[j] % half, 0, 0))
    table = pl.BlockSpec((t, HEAD_WIDTH), lambda j, s: (0, 0))
    return pl.pallas_call(
        functools.partial(project_kernel, cw // HEAD_WIDTH, half),
        grid_spec=pltpu.PrefetchScalarGridSpec(
            num_scalar_prefetch=1,
            grid=(m,),
            in_specs=[pl.BlockSpec((t, d), lambda j, s: (0, 0))] + [w_spec] * 4 + [table] * 2,
            out_specs=pl.BlockSpec((t, cw), lambda j, s: (0, j)),
        ),
        out_shape=jax.ShapeDtypeStruct((t, m * cw), bf16),
        compiler_params=params(24),
        cost_estimate=cost(2 * t * d * m * cw, 2 * d * m * cw),
        name="project",
    )(slot_of, h, *w_a, *w_b, cos, sin)


def project_back_kernel(half, chunk_ref, h_ref, g_ref, an_ref, af_ref, bn_ref, bf_ref, dh_ref, gn_ref, gf_ref):
    j = pl.program_id(0)
    cut = an_ref.shape[1]

    @pl.when(j == 0)
    def _():
        dh_ref[...] = jnp.zeros_like(dh_ref)

    def run(a_ref, b_ref, gw_ref):
        dh_ref[:, :cut] += dot_nt(g_ref[...], a_ref[0])
        dh_ref[:, cut:] += dot_nt(g_ref[...], b_ref[0])
        gw_ref[0] = dot_tn(h_ref[...], g_ref[...]).astype(bf16)

    pl.when(j < half)(lambda: run(af_ref, bf_ref, gf_ref))
    pl.when(j >= half)(lambda: run(an_ref, bn_ref, gn_ref))


def project_back(chunk_of, h, grad, w_a, w_b):
    half, cut, cw = w_a[0].shape
    t, d = h.shape
    m = 2 * half
    first = lambda j, c: (jnp.minimum(j, half - 1), 0, 0)
    second = lambda j, c: (jnp.maximum(j - half, 0), 0, 0)
    near, far = pl.BlockSpec((1, cut, cw), second), pl.BlockSpec((1, cut, cw), first)
    return pl.pallas_call(
        functools.partial(project_back_kernel, half),
        grid_spec=pltpu.PrefetchScalarGridSpec(
            num_scalar_prefetch=1,
            grid=(m,),
            in_specs=[
                pl.BlockSpec((t, d), lambda j, c: (0, 0)),
                pl.BlockSpec((t, cw), lambda j, c: (0, c[(j + half) % m])),
                near,
                far,
                near,
                far,
            ],
            out_specs=[
                pl.BlockSpec((t, d), lambda j, c: (0, 0)),
                pl.BlockSpec((1, d, cw), second),
                pl.BlockSpec((1, d, cw), first),
            ],
        ),
        out_shape=[
            jax.ShapeDtypeStruct((t, d), f32),
            jax.ShapeDtypeStruct((half, d, cw), bf16),
            jax.ShapeDtypeStruct((half, d, cw), bf16),
        ],
        compiler_params=params(32),
        cost_estimate=cost(4 * t * d * m * cw, 4 * d * m * cw),
        name="project_back",
    )(chunk_of, h, grad, *w_a, *w_b)


def visible(rank, shape, dim):
    slot = lax.shift_right_logical(lax.broadcasted_iota(jnp.int32, shape, dim), BLK.bit_length() - 1)
    return (slot ^ rank) <= rank


def attend_kernel(rank_ref, q_ref, k_ref, v_ref, out_ref):
    s = dot_nt(q_ref[...], k_ref[...]) * score_scale
    s = jnp.where(visible(rank_ref[0], s.shape, 1), s, mask_fill)
    e = jnp.exp(s - jnp.max(s, 1, keepdims=True))
    p = (e / jnp.sum(e, 1, keepdims=True)).astype(bf16)
    out_ref[...] = dot_nn(p, v_ref[...]).astype(bf16)


def attend(rank, qkv, kv):
    t, rows = qkv.shape[0], kv.shape[0]
    return pl.pallas_call(
        attend_kernel,
        grid_spec=pltpu.PrefetchScalarGridSpec(
            num_scalar_prefetch=1,
            grid=(QUERY_HEADS,),
            in_specs=[
                pl.BlockSpec((t, HEAD_WIDTH), lambda j, s: (0, j)),
                pl.BlockSpec((rows, HEAD_WIDTH), lambda j, s: (0, j // group_heads)),
                pl.BlockSpec((rows, HEAD_WIDTH), lambda j, s: (0, KEY_VALUE_HEADS + j // group_heads)),
            ],
            out_specs=pl.BlockSpec((t, HEAD_WIDTH), lambda j, s: (0, j)),
        ),
        out_shape=jax.ShapeDtypeStruct((t, query_columns), bf16),
        compiler_params=params(40),
        cost_estimate=cost(4 * t * rows * query_columns, 4 * t * query_columns, t * rows * QUERY_HEADS),
        name="attend",
    )(rank, qkv, kv, kv)


def attend_back_kernel(rank_ref, q_ref, k_ref, v_ref, g_ref, cos_ref, sin_ref, dq_ref, dkv_ref, dk_acc, dv_acc):
    j = pl.program_id(0)
    q, k, g = q_ref[...], k_ref[...], g_ref[...]
    s = dot_nt(k, q) * score_scale
    s = jnp.where(visible(rank_ref[0], s.shape, 0), s, mask_fill)
    e = jnp.exp(s - jnp.max(s, 0, keepdims=True))
    p = e / jnp.sum(e, 0, keepdims=True)
    pb = p.astype(bf16)
    dp = dot_nt(v_ref[...], g)
    delta = jnp.sum(p * dp, 0, keepdims=True)
    ds = (p * (dp - delta)).astype(bf16)
    dq = dot_tn(ds, k) * score_scale
    dq_ref[...] = (dq * cos_ref[...] - pltpu.roll(dq, HEAD_WIDTH // 2, 1) * sin_ref[...]).astype(bf16)

    @pl.when(j % group_heads == 0)
    def _():
        dk_acc[...] = jnp.zeros_like(dk_acc)
        dv_acc[...] = jnp.zeros_like(dv_acc)

    dk_acc[...] += dot_nn(ds, q) * score_scale
    dv_acc[...] += dot_nn(pb, g)

    @pl.when(j % group_heads == group_heads - 1)
    def _():
        dkv_ref[0] = dk_acc[...].astype(bf16)
        dkv_ref[1] = dv_acc[...].astype(bf16)


def attend_back(rank, qkv, kv, grad, cos, sin):
    t, rows = qkv.shape[0], kv.shape[0]
    return pl.pallas_call(
        attend_back_kernel,
        grid_spec=pltpu.PrefetchScalarGridSpec(
            num_scalar_prefetch=1,
            grid=(QUERY_HEADS,),
            in_specs=[
                pl.BlockSpec((t, HEAD_WIDTH), lambda j, s: (0, j)),
                pl.BlockSpec((rows, HEAD_WIDTH), lambda j, s: (0, j // group_heads)),
                pl.BlockSpec((rows, HEAD_WIDTH), lambda j, s: (0, KEY_VALUE_HEADS + j // group_heads)),
                pl.BlockSpec((t, HEAD_WIDTH), lambda j, s: (0, j)),
                pl.BlockSpec((t, HEAD_WIDTH), lambda j, s: (0, 0)),
                pl.BlockSpec((t, HEAD_WIDTH), lambda j, s: (0, 0)),
            ],
            out_specs=[
                pl.BlockSpec((t, HEAD_WIDTH), lambda j, s: (0, j)),
                pl.BlockSpec((2, rows, HEAD_WIDTH), lambda j, s: (0, 0, j // group_heads)),
            ],
            scratch_shapes=[pltpu.VMEM((rows, HEAD_WIDTH), f32)] * 2,
        ),
        out_shape=[
            jax.ShapeDtypeStruct((t, query_columns), bf16),
            jax.ShapeDtypeStruct((2, rows, key_columns), bf16),
        ],
        compiler_params=params(56),
        cost_estimate=cost(10 * t * rows * query_columns, 8 * t * query_columns, t * rows * QUERY_HEADS),
        name="attend_back",
    )(rank, qkv, kv, kv, grad, cos, sin)


def experts_kernel(
    chunk_ref, h_ref, z_ref, gn_ref, gf_ref, un_ref, uf_ref, wd_ref,
    a_ref, dg_ref, du_ref, eo_ref, dh_ref, weights, eo_acc, dh_acc, dgate_acc, sems,
):
    per, fc, d = weights.shape[2:]
    ct = per * fc

    def copies(side):
        moves = [
            pltpu.make_async_copy((gn_ref, gf_ref)[side], weights.at[side, 0], sems.at[side, 0]),
            pltpu.make_async_copy((un_ref, uf_ref)[side], weights.at[side, 1], sems.at[side, 1]),
        ]
        for k in range(per):
            moves.append(
                pltpu.make_async_copy(
                    wd_ref.at[chunk_ref[side * per + k]], weights.at[side, 2, k], sems.at[side, 2 + k]
                )
            )
        return moves

    for side in range(2):
        for move in copies(side):
            move.start()
    t = z_ref.shape[0]
    gates_high = h_ref[t:, :t]
    gates_low = h_ref[t:, t : 2 * t]
    for side in range(2):
        moves = copies(side)
        slot_row = lax.broadcasted_iota(jnp.int32, (EXTRA, ct), 0)
        slot_col = lax.broadcasted_iota(jnp.int32, (EXTRA, ct), 1) + side * ct
        low = slot_row * fc
        pick = jnp.where((slot_col >= low) & (slot_col < low + fc), 1.0, 0.0).astype(bf16)
        wide = dot_tn(gates_high, pick) + dot_tn(gates_low, pick)
        moves[0].wait()
        wg = weights[side, 0].reshape(ct, d)
        g = dot_nt(h_ref[:t], wg)
        moves[1].wait()
        wu = weights[side, 1].reshape(ct, d)
        u = dot_nt(h_ref[:t], wu)
        for move in moves[2:]:
            move.wait()
        wd = weights[side, 2].reshape(ct, d)
        e = dot_nt(z_ref[...], wd)
        sig = 1.0 / (1.0 + jnp.exp(-g))
        swish = g * sig
        a = swish * u
        da = e * wide
        at = slice(side * ct, (side + 1) * ct)
        ab = (a * wide).astype(bf16)
        dg = (da * u * (sig * (1.0 + g * (1.0 - sig)))).astype(bf16)
        du = (da * swish).astype(bf16)
        a_ref[:, at] = ab
        dg_ref[:, at] = dg
        du_ref[:, at] = du
        dgate = dot_nt(pick, (a * e).astype(bf16))
        if side == 0:
            dgate_acc[...] = dgate
            dh_acc[...] = dot_nn(dg, wg)
            dh_acc[...] += dot_nn(du, wu)
            eo_acc[...] = dot_nn(ab, wd)
        else:
            dgate = dgate_acc[...] + dgate
            high = dgate.astype(dh_ref.dtype)
            dh_ref[t:] = jnp.zeros((EXTRA, d), dh_ref.dtype)
            dh_ref[t:, :t] = high
            dh_ref[t:, t : 2 * t] = (dgate - high.astype(f32)).astype(dh_ref.dtype)
            dh_acc[...] += dot_nn(dg, wg)
            dh_ref[:t] = (dh_acc[...] + dot_nn(du, wu)).astype(dh_ref.dtype)
            eo_ref[...] = (eo_acc[...] + dot_nn(ab, wd)).astype(eo_ref.dtype)


def experts(chunk_of, h, z, wg, wu, wd, sent_type):
    t, d = z.shape
    per, fc = wg[0].shape[0], wg[0].shape[1]
    width = 2 * per * fc
    vmem, hbm = pl.BlockSpec(memory_space=pltpu.VMEM), pl.BlockSpec(memory_space=pl.ANY)
    return pl.pallas_call(
        experts_kernel,
        in_specs=[pl.BlockSpec(memory_space=pltpu.SMEM)] + [vmem] * 2 + [hbm] * 5,
        out_specs=[vmem] * 5,
        out_shape=[
            jax.ShapeDtypeStruct((t, width), bf16),
            jax.ShapeDtypeStruct((t, width), bf16),
            jax.ShapeDtypeStruct((t, width), bf16),
            jax.ShapeDtypeStruct((t, d), sent_type),
            jax.ShapeDtypeStruct((t + EXTRA, d), sent_type),
        ],
        scratch_shapes=[
            pltpu.VMEM((2, 3, per, fc, d), bf16),
            pltpu.VMEM((t, d), f32),
            pltpu.VMEM((t, d), f32),
            pltpu.VMEM((EXTRA, t), f32),
            pltpu.SemaphoreType.DMA((2, 2 + per)),
        ],
        compiler_params=params(48),
        cost_estimate=cost(12 * t * d * width, 6 * d * width),
        name="experts",
    )(chunk_of, h, z, *wg, *wu, wd)


def expert_grads_kernel(n, fc, *refs):
    a, dg, du = refs[:n], refs[n : 2 * n], refs[2 * n : 3 * n]
    h, z, out_ref = refs[3 * n : 4 * n], refs[4 * n : 5 * n], refs[5 * n]
    per = out_ref.shape[0]
    for which, (left, right) in enumerate(((dg, h), (du, h), (a, z))):
        total = dot_tn(left[0][...], right[0][...])
        for s in range(1, n):
            total += dot_tn(left[s][...], right[s][...])
        out_ref[:, which] = total.astype(bf16).reshape(per, fc, total.shape[-1])


def expert_grads(side, fc, a, dg, du, h, z):
    n = len(a)
    t, width = a[0].shape
    width = width // 2
    d = h[0].shape[1]
    ct = min(width, 384)
    per = ct // fc
    steps = width // ct
    tile = pl.BlockSpec((t, ct), lambda j: (0, side * steps + j))
    rows = pl.BlockSpec((t, d), lambda j: (0, 0))
    if width % HEAD_WIDTH:
        a, dg, du = ([x[:, side * width : (side + 1) * width] for x in xs] for xs in (a, dg, du))
        tile = pl.BlockSpec((t, width), lambda j: (0, 0))
    return pl.pallas_call(
        functools.partial(expert_grads_kernel, n, fc),
        grid=(steps,),
        in_specs=[tile] * (3 * n) + [rows] * (2 * n),
        out_specs=pl.BlockSpec((per, 3, fc, d), lambda j: (j, 0, 0, 0)),
        out_shape=jax.ShapeDtypeStruct((width // fc, 3, fc, d), bf16),
        compiler_params=params(58),
        cost_estimate=cost(6 * n * t * d * width, 6 * d * width),
        name="expert_grads",
    )(*a, *dg, *du, *h, *z)


def join_kernel(half, slot_ref, *refs):
    out_ref = refs[-1]
    near = slot_ref[pl.program_id(0)] < half

    def run(side):
        at = 0
        for k in range(side, len(refs) - 1, 2):
            block = refs[k][0]
            rows = block.shape[0]
            if out_ref.ndim == 4:
                out_ref[at : at + rows, 0] = block.astype(out_ref.dtype)
            else:
                out_ref[0, at : at + rows] = block.astype(out_ref.dtype)
            at += rows

    pl.when(near)(lambda: run(0))
    pl.when(jnp.logical_not(near))(lambda: run(1))


def join(slot_of, parts, dtype, spread_out=False):
    half = parts[0][0].shape[0]
    m = 2 * half
    tail = parts[0][0].shape[2:]
    rows = sum(near.shape[1] for near, far in parts)
    zeros = (0,) * len(tail)
    specs, flat = [], []
    for pair in parts:
        for x in pair:
            specs.append(pl.BlockSpec((1,) + x.shape[1:], lambda j, s: (s[j] % half, 0) + zeros))
            flat.append(x)
    if spread_out:
        out_spec = pl.BlockSpec((rows, 1) + tail, lambda j, s: (0, j) + zeros)
        shape = (rows, m) + tail
    else:
        out_spec = pl.BlockSpec((1, rows) + tail, lambda j, s: (j, 0) + zeros)
        shape = (m, rows) + tail
    return pl.pallas_call(
        functools.partial(join_kernel, half),
        grid_spec=pltpu.PrefetchScalarGridSpec(
            num_scalar_prefetch=1, grid=(m,), in_specs=specs, out_specs=out_spec
        ),
        out_shape=jax.ShapeDtypeStruct(shape, dtype),
        compiler_params=params(24),
        cost_estimate=cost(0, 6 * math.prod(shape)),
        name="join",
    )(slot_of, *flat)


def split_kernel(half, chunk_ref, in_ref, near_ref, far_ref):
    j = pl.program_id(0)

    @pl.when(j < half)
    def _():
        far_ref[0] = in_ref[:, 0]

    @pl.when(j >= half)
    def _():
        near_ref[0] = in_ref[:, 0]


def split(chunk_of, x):
    n, m, c, d = x.shape
    half = m // 2
    return pl.pallas_call(
        functools.partial(split_kernel, half),
        grid_spec=pltpu.PrefetchScalarGridSpec(
            num_scalar_prefetch=1,
            grid=(m,),
            in_specs=[pl.BlockSpec((n, 1, c, d), lambda j, s: (0, s[(j + half) % m], 0, 0))],
            out_specs=[
                pl.BlockSpec((1, n, c, d), lambda j, s: (jnp.maximum(j - half, 0), 0, 0, 0)),
                pl.BlockSpec((1, n, c, d), lambda j, s: (jnp.minimum(j, half - 1), 0, 0, 0)),
            ],
        ),
        out_shape=[jax.ShapeDtypeStruct((half, n, c, d), x.dtype)] * 2,
        compiler_params=params(16),
        cost_estimate=cost(0, 4 * x.size),
        name="split",
    )(chunk_of, x)


def columns_kernel(half, counts, slot_ref, near_ref, far_ref, *out_refs):
    j = pl.program_id(0)
    near = slot_ref[j] < half
    at = 0
    for count, out_ref in zip(counts, out_refs):
        mine = (j >= at) & (j < at + count)

        @pl.when(mine & near)
        def _(out_ref=out_ref):
            out_ref[...] = near_ref[0].astype(f32)

        @pl.when(mine & jnp.logical_not(near))
        def _(out_ref=out_ref):
            out_ref[...] = far_ref[0].astype(f32)

        at += count


def columns(slot_of, near, far, widths):
    half, rows, cw = near.shape
    counts = [w // cw for w in widths]
    specs, at = [], 0
    for count in counts:
        specs.append(
            pl.BlockSpec((rows, cw), lambda j, s, at=at, top=count - 1: (0, jnp.clip(j - at, 0, top)))
        )
        at += count
    in_spec = pl.BlockSpec((1, rows, cw), lambda j, s: (s[j] % half, 0, 0))
    return pl.pallas_call(
        functools.partial(columns_kernel, half, counts),
        grid_spec=pltpu.PrefetchScalarGridSpec(
            num_scalar_prefetch=1, grid=(2 * half,), in_specs=[in_spec] * 2, out_specs=specs
        ),
        out_shape=[jax.ShapeDtypeStruct((rows, w), f32) for w in widths],
        compiler_params=params(16),
        cost_estimate=cost(0, 12 * near.size),
        name="columns",
    )(slot_of, near, far)


def arrange_kernel(n, fc, rc, rank_ref, *refs):
    slots, (gate_ref, up_ref, a_ref, b_ref) = refs[:n], refs[n:]
    dl = slots[0].shape[1]

    def run(rank):
        for q in range(n):
            block = slots[q ^ rank]
            gate_ref[:, q * dl : (q + 1) * dl] = block[:fc]
            up_ref[:, q * dl : (q + 1) * dl] = block[fc : 2 * fc]
            out_ref = (a_ref, b_ref)[q // (n // 2)]
            for b in range(n):
                at = 2 * fc + b * rc
                out_ref[q % (n // 2), :, b * dl : (b + 1) * dl] = block[at : at + rc]

    for rank in range(n):
        pl.when(rank_ref[0] == rank)(functools.partial(run, rank))


def arrange(rank, slots, fc, rc):
    n, d = len(slots), len(slots) * slots[0].shape[1]
    vmem = pl.BlockSpec(memory_space=pltpu.VMEM)
    return pl.pallas_call(
        functools.partial(arrange_kernel, n, fc, rc),
        in_specs=[pl.BlockSpec(memory_space=pltpu.SMEM)] + [vmem] * n,
        out_specs=[vmem] * 4,
        out_shape=[jax.ShapeDtypeStruct((fc, d), bf16)] * 2 + [jax.ShapeDtypeStruct((n // 2, rc, d), bf16)] * 2,
        compiler_params=params(16),
        cost_estimate=cost(0, 8 * fc * d),
        name="arrange",
    )(rank, *slots)


class Rounds:
    def __init__(self):
        self.gate, self.made, self.later = (), [], []

    def enter(self, x):
        return after(x, *self.gate) if self.gate else x

    def leave(self, *xs):
        self.made.extend(xs)
        return xs[0]

    def leave_late(self, *xs):
        self.later.extend(xs)
        return xs[0]

    def turn(self):
        self.gate, self.made, self.later = tuple(self.made), self.later, []


class Along:
    def __init__(self, rounds):
        self.rounds = rounds
        self.n, self.m = lax.axis_size("cp"), lax.axis_size("dp")
        self.r, self.i = lax.axis_index("cp"), lax.axis_index("dp")
        self.bits = self.m.bit_length() - 1
        assert 1 << self.bits == self.m and self.bits > 1
        self.inner = self.bits - 1
        slots = jnp.arange(self.m, dtype=jnp.int32)
        self.chunk_of = self.i ^ (((slots & (self.m // 2 - 1)) << 1) | (slots >> self.inner))
        offset = slots ^ self.i
        self.slot_of = (offset >> 1) | ((offset & 1) << self.inner)

    def send(self, x, axis, pairs, late=False):
        leave = self.rounds.leave_late if late else self.rounds.leave
        return leave(lax.ppermute(self.rounds.enter(x), axis, pairs))

    def swap(self, x, bit, late=False):
        mask = 1 if bit == self.inner else 2 << bit
        return self.send(x, "dp", [(k, k ^ mask) for k in range(self.m)], late)

    def cross(self, x, s, keep=None, late=False):
        pairs = [(k, k ^ s) for k in range(self.n)]
        return self.send(x, "cp", [p for p in pairs if keep is None or keep(*p)], late)

    def orders(self):
        up = list(range(self.inner))
        return up, up[::-1]

    def pieces(self, x, s):
        return lax.dynamic_index_in_dim(x, self.r ^ s, 0, keepdims=False)

    def scatter_cp(self, x):
        return [self.pieces(x, 0)] + [self.cross(self.pieces(x, s), s) for s in range(1, self.n)]

    def ranked(self, slots):
        for bit in range(self.n.bit_length() - 1):
            turned = (self.r >> bit & 1) == 1
            slots = [jnp.where(turned, slots[k ^ 1 << bit], slots[k]) for k in range(self.n)]
        return jnp.stack(slots)

    def gather_cp(self, x):
        return [x] + [self.cross(x, s) for s in range(1, self.n)]


class Gather:
    def __init__(self, along, *xs):
        self.along, self.parts, self.at = along, [{0: x} for x in xs], 0

    def step(self, late=False):
        for k, held in enumerate(self.parts):
            bit = self.along.orders()[k % 2][self.at]
            slots = sorted(held)
            got = self.along.swap(jnp.stack([held[h] for h in slots]), bit, late)
            for p, h in enumerate(slots):
                held[h | 1 << bit] = got[p]
        self.at += 1

    def rest(self, late=False):
        while self.at < self.along.inner:
            self.step(late)

    def finish(self, late=False):
        self.rest(late)
        near = [jnp.stack([held[h] for h in sorted(held)]) for held in self.parts]
        return [(x, self.along.swap(x, self.along.inner, late)) for x in near]


class Reduce:
    def __init__(self, along, far):
        self.along, self.at = along, 0
        self.got = along.swap(far, along.inner)

    def add(self, near):
        cut = near.shape[1] // 2
        self.parts = [
            {h: near[h, at].astype(f32) + self.got[h, at].astype(f32) for h in range(self.along.m // 2)}
            for at in (slice(0, cut), slice(cut, None))
        ]

    def step(self, late=False):
        for k, held in enumerate(self.parts):
            bit = self.along.orders()[1 - k][self.at]
            sent = jnp.stack([held[h].astype(bf16) for h in sorted(held) if h >> bit & 1])
            more = self.along.swap(sent, bit, late)
            kept = [h for h in sorted(held) if not h >> bit & 1]
            self.parts[k] = {h: held[h] + more[p].astype(f32) for p, h in enumerate(kept)}
        self.at += 1

    def rest(self, late=False):
        while self.at < self.along.inner:
            self.step(late)

    def finish(self):
        self.rest()
        return jnp.concatenate([p[0] for p in self.parts], 0).astype(bf16)


class Relay:
    inside, outside, turned = [(1, 2), (2, 1)], [(1, 0), (2, 3)], [(0, 1), (3, 2)]

    def __init__(self, along, x):
        self.along, self.x, self.four = along, x, along.n == 4

    def one(self):
        self.first = self.along.cross(self.x, 1)

    def middle(self):
        if self.four:
            self.third = self.along.send(self.x, "cp", self.inside)

    def two(self, late=False):
        self.second = self.along.cross(self.x, 2, late=late)

    def ends(self):
        along = self.along
        if self.four:
            outer = along.send(self.second, "cp", self.outside)
            self.third = [jnp.where((along.r == 1) | (along.r == 2), self.third, outer)]
        else:
            self.third = [along.cross(self.x, s) for s in range(3, along.n)]

    def slots(self):
        return [self.x, self.first, self.second, *self.third]


def norm_forward(values, gain_vec):
    inverse = lax.rsqrt(jnp.mean(values * values, -1, keepdims=True) + norm_eps)
    scaled = values * inverse
    return (scaled * gain_vec, scaled, inverse)


def norm_backward(gradient, gain_vec, scaled, inverse):
    gain_grad = jnp.sum(gradient * scaled, 0)
    inner_vals = gradient * gain_vec
    return (
        inverse * (inner_vals - scaled * jnp.mean(inner_vals * scaled, -1, keepdims=True)),
        gain_grad,
    )


def rotary(positions):
    half = HEAD_WIDTH // 2
    frequency = rope_base ** (-2.0 * jnp.arange(half, dtype=f32) / HEAD_WIDTH)
    angles = positions.astype(f32)[:, None] * frequency[None, :]
    cos, sin = jnp.cos(angles), jnp.sin(angles)
    return jnp.concatenate([cos, cos], 1), jnp.concatenate([-sin, sin], 1)


def local(
    tokens, routes, out_grad, norm_attn, w_query, key_weight, value_weight, w_out,
    norm_mix, w_router, w_gate, w_up, w_down,
):
    rounds = Rounds()
    along = Along(rounds)
    n, m, r, i = along.n, along.m, along.r, along.i
    t, d = tokens.shape[1], tokens.shape[2]
    assert t == BLK
    dl, ff, fs = w_query.shape[0], w_gate.shape[2], w_down.shape[1]
    sub = m // EXPERTS
    fc = fs // sub
    rc = dl // m
    inputs = tokens[0].astype(f32)
    route_rows = routes[0]
    dz = out_grad[0]
    up = lambda a, b: b > a
    down = lambda a, b: b < a

    w_qkv = jnp.concatenate([w_query, key_weight, value_weight], 1)
    cw = w_qkv.shape[1] // m
    small = jnp.concatenate([norm_attn[None], norm_mix[None], w_router.T], 0).reshape(-1)
    tail = -(-small.shape[0] // (16 * cw)) * 16
    small = jnp.concatenate([small, jnp.zeros((tail * cw - small.shape[0],), bf16)]).reshape(tail, cw)
    sent = jnp.concatenate([lax.dynamic_slice_in_dim(w_qkv, i * cw, cw, 1), small], 0)
    got = along.ranked(along.gather_cp(sent))
    own_qkv = got[:, :dl].reshape(d, cw)
    small = got[:, dl:].reshape(n, tail * cw)[:, : (2 + EXPERTS) * dl].reshape(n, 2 + EXPERTS, dl)
    small = jnp.swapaxes(small, 0, 1).reshape(2 + EXPERTS, d)
    gain_one, gain_two = small[0].astype(f32), small[1].astype(f32)
    router = small[2:]
    flipped = [
        lax.dynamic_index_in_dim(w, i // sub, 0, keepdims=False).T.reshape(n, sub, fc, dl)
        for w in (w_gate, w_up)
    ]
    flipped = lax.dynamic_index_in_dim(jnp.stack(flipped, 1), i % sub, 2, keepdims=False).reshape(n, 2 * fc, dl)
    out_rows = lax.dynamic_slice_in_dim(w_out, i * rc, rc, 0).reshape(rc, n, dl)
    out_rows = jnp.swapaxes(out_rows, 0, 1).reshape(1, n * rc, dl)
    flipped = jnp.concatenate([flipped, jnp.broadcast_to(out_rows, (n, n * rc, dl))], 1)
    flipped = rounds.leave(flipped)
    cos, sin = rotary(r * t + jnp.arange(t, dtype=jnp.int32))
    rounds.leave(cos, sin)

    rounds.turn()
    qkv_gather = Gather(along, own_qkv[: d // 2], own_qkv[d // 2 :])
    qkv_gather.step()
    mix = [along.pieces(flipped, 0), along.cross(along.pieces(flipped, 1), 1)]
    normed_one, scaled_one, inverse_one = norm_forward(inputs, gain_one)
    h1 = rounds.leave(normed_one.astype(bf16))
    rounds.turn()
    qkv_gather.rest()
    mix.append(along.cross(along.pieces(flipped, 2), 2))
    rounds.turn()
    qkv_a, qkv_b = qkv_gather.finish()
    mix.extend(along.cross(along.pieces(flipped, s), s, late=True) for s in range(3, n))
    rounds.turn()
    rank = r.reshape(1)
    qkv = rounds.leave(project(along.slot_of, rounds.enter(h1), qkv_a, qkv_b, cos, sin))
    rounds.turn()

    own_kv = qkv[:, query_columns:]
    kv = jnp.concatenate([own_kv] + [along.cross(own_kv, s, up) for s in range(1, n)], 0)
    if dl % HEAD_WIDTH == 0:
        gate_rows, up_rows, out_first, out_second = arrange(rank, [rounds.enter(x) for x in mix], fc, rc)
    else:
        got = along.ranked(mix)
        gate_rows, up_rows = jnp.swapaxes(got[:, : 2 * fc], 0, 1).reshape(2, fc, d)
        own_out = jnp.swapaxes(got[:, 2 * fc :].reshape(n, n, rc, dl), 1, 2).reshape(n, rc, d)
        out_first, out_second = own_out[: n // 2], own_out[n // 2 :]
    out_gather = Gather(along, out_first, out_second)
    out_gather.step()
    mix_gather = Gather(along, gate_rows, up_rows)
    mix_gather.step()
    rounds.turn()
    z_relay = Relay(along, dz)
    z_relay.two()
    out_gather.rest()
    mix_gather.rest()
    ob = rounds.leave(attend(rank, qkv, rounds.enter(kv)))
    rounds.turn()
    z_relay.one()
    z_relay.middle()
    out_a, out_b = out_gather.finish()
    wg, wu = mix_gather.finish()
    wd = w_down.reshape(m, fc, d)
    full_out = join(along.slot_of, [out_a, out_b], bf16, True).reshape(n * dl, d)

    middle = inputs + dot_nn(rounds.enter(ob), full_out)
    normed_two, scaled_two, inverse_two = norm_forward(middle, gain_two)
    h2 = normed_two.astype(bf16)
    logits = dot_nt(h2, router)
    experts_range = jnp.arange(EXPERTS, dtype=jnp.int32)
    route_flags = (route_rows[:, :, None] == experts_range).astype(f32)
    chosen = jnp.sum(logits[:, None, :] * route_flags, -1)
    raised = jnp.exp(chosen - jnp.max(chosen, -1, keepdims=True))
    gate_vals = raised / jnp.sum(raised, -1, keepdims=True)
    slot_flags = (route_rows[:, :, None] == along.chunk_of // sub).astype(f32)
    gates = jnp.sum(gate_vals[:, :, None] * slot_flags, 1).T
    gates = jnp.concatenate([gates, jnp.zeros((EXTRA - m, t), f32)], 0)
    gates_high = gates.astype(bf16)
    gates_low = (gates - gates_high.astype(f32)).astype(bf16)
    gates = jnp.concatenate([gates_high, gates_low, jnp.zeros((EXTRA, d - 2 * t), bf16)], 1)
    h_sent = rounds.leave(jnp.concatenate([h2, gates], 0))
    rounds.turn()

    h_relay = Relay(along, h_sent)
    h_relay.one()
    h_relay.middle()

    def run(h, z, sent_type=bf16):
        results = experts(along.chunk_of, rounds.enter(h), z, wg, wu, wd, sent_type)
        rounds.leave(*results)
        return results

    done = [run(h_sent, dz, f32)]
    rounds.turn()
    h_relay.two()
    z_relay.ends()
    done.append(run(h_relay.first, z_relay.first))
    rounds.turn()
    h_relay.ends()
    done.append(run(h_relay.second, z_relay.second))
    rounds.turn()
    h_slots, z_slots = h_relay.slots(), z_relay.slots()
    h2_back = done[0][4] + along.cross(done[1][4], 1).astype(f32)
    done.extend(run(h_slots[s], z_slots[s]) for s in range(3, n))
    rounds.turn()
    triples = [[rounds.enter(x[k]) for x in done] for k in range(3)]
    second = done[2][4]
    if n == 4:
        h2_back = h2_back + along.send(done[3][4], "cp", Relay.inside).astype(f32)
        second = (second.astype(f32) + along.send(done[3][4], "cp", Relay.turned).astype(f32)).astype(bf16)
    else:
        for s in range(3, n):
            h2_back = h2_back + along.cross(done[s][4], s).astype(f32)
    mix_far = rounds.leave(expert_grads(1, fc, *triples, h_slots, z_slots).reshape(m // 2, 3 * fc, d))
    rounds.turn()
    h2_back = h2_back + along.cross(second, 2).astype(f32)
    mix_reduce = Reduce(along, mix_far)
    triples = [[rounds.enter(x) for x in xs] for xs in triples]
    mix_near = rounds.leave(expert_grads(0, fc, *triples, h_slots, z_slots).reshape(m // 2, 3 * fc, d))
    rounds.turn()
    mix_reduce.add(mix_near)
    mix_reduce.step()

    mixed = done[0][3] + along.cross(done[1][3], 1).astype(f32)
    second_out = done[2][3]
    if n == 4:
        mixed = mixed + along.send(done[3][3], "cp", Relay.inside).astype(f32)
        second_out = second_out.astype(f32) + along.send(done[3][3], "cp", Relay.turned).astype(f32)
        second_out = second_out.astype(bf16)
    h2_back = rounds.enter(h2_back)
    slot_gate_grad = h2_back[t : t + m, :t] + h2_back[t : t + m, t : 2 * t]
    gate_grad = jnp.sum(slot_gate_grad.T[:, None, :] * slot_flags, -1)
    weighted = gate_vals * gate_grad
    chosen_grad = weighted - gate_vals * jnp.sum(weighted, -1, keepdims=True)
    logit_grad = jnp.sum(chosen_grad[:, :, None] * route_flags, 1).astype(bf16)
    router_grad = dot_tn(logit_grad, h2)
    h2_grad = h2_back[:t] + dot_nn(logit_grad, router)
    middle_norm_grad, gain_two_grad = norm_backward(h2_grad, gain_two, scaled_two, inverse_two)
    middle_grad = dz.astype(f32) + middle_norm_grad
    branch = middle_grad.astype(bf16)

    dob = dot_nt(branch, full_out).astype(bf16)
    out_grads = dot_tn(ob, branch).astype(bf16)
    out_near, out_far = split(along.chunk_of, out_grads.reshape(n, m, rc, d))
    dq, dkv = attend_back(rank, qkv, kv, dob, cos, sin)
    rounds.leave(dkv, out_near, out_far)
    rounds.turn()
    dkv_own = dkv[:, :t].astype(f32)
    for s in range(1, n):
        dkv_own = dkv_own + along.cross(dkv[:, s * t : (s + 1) * t], s, down).astype(f32)
    mix_reduce.rest()
    out_reduce = Reduce(along, out_far)
    rounds.turn()
    out_reduce.add(out_near)
    out_reduce.step()
    dkv_own = rounds.enter(dkv_own)
    dk = dkv_own[0].reshape(t, KEY_VALUE_HEADS, HEAD_WIDTH)
    half = HEAD_WIDTH // 2
    dk = dk * cos[:, None] - jnp.concatenate([dk[..., half:], dk[..., :half]], -1) * sin[:, None]
    dqkv = jnp.concatenate([dq, dk.reshape(t, key_columns).astype(bf16), dkv_own[1].astype(bf16)], 1)
    own_mix = mix_reduce.finish()
    back = [lax.dynamic_slice_in_dim(own_mix[: 2 * fc], (r ^ s) * dl, dl, 1) for s in range(n)]
    back = [back[0]] + [along.cross(back[s], s) for s in range(1, n)]
    own_down = own_mix[2 * fc :]
    down_gather = Gather(along, own_down[: fc // 2], own_down[fc // 2 :])
    down_gather.step()
    h1_grad, qkv_near, qkv_far = project_back(along.chunk_of, h1, dqkv, qkv_a, qkv_b)
    rounds.leave(h1_grad, qkv_near, qkv_far)
    rounds.turn()

    def sum_cp(x):
        return functools.reduce(jnp.add, [y.astype(f32) for y in along.scatter_cp(x)]).astype(bf16)

    qkv_reduce = Reduce(along, qkv_far)
    out_reduce.rest()
    down_gather.rest()
    input_norm_grad, gain_one_grad = norm_backward(h1_grad, gain_one, scaled_one, inverse_one)
    input_grad = (middle_grad + input_norm_grad).astype(bf16)[None]
    small_grads = jnp.concatenate([gain_one_grad[None], gain_two_grad[None], router_grad], 0)
    small_grads = rounds.leave(jnp.transpose(small_grads.reshape(2 + EXPERTS, n, dl), (1, 0, 2)))
    back = along.ranked(back).reshape(n, 2, fc, dl)
    back = rounds.leave(jnp.transpose(back, (1, 3, 0, 2)).reshape(2, dl, n * fc))
    rounds.turn()
    qkv_reduce.add(qkv_near)
    qkv_reduce.step()
    own_out = sum_cp(out_reduce.finish())
    small_grads = functools.reduce(jnp.add, along.scatter_cp(small_grads))
    rounds.turn()
    qkv_reduce.rest()
    back_gather = Gather(along, back[0], back[1])
    back_gather.step()
    out_gather = Gather(along, own_out)
    out_gather.step()
    small_grads = small_grads + along.swap(small_grads, along.inner)
    mixed = mixed + along.cross(second_out, 2).astype(f32)
    rounds.turn()
    back_gather.rest()
    out_gather.rest()
    own_qkv = sum_cp(qkv_reduce.finish().reshape(n, dl, cw))
    small_grads = small_grads + along.swap(small_grads, 0)
    if n != 4:
        for s in range(3, n):
            mixed = mixed + along.cross(done[s][3], s).astype(f32)
    rounds.turn()
    qkv_gather = Gather(along, own_qkv)
    qkv_gather.step()
    back_slots = back_gather.finish()
    (out_slots,) = out_gather.finish()
    down_a, down_b = down_gather.finish()
    for bit in range(1, along.inner):
        small_grads = small_grads + along.swap(small_grads, bit)
    output = (middle + mixed).astype(bf16)[None]
    rounds.turn()
    qkv_gather.rest()
    grad_w_down = join(along.slot_of, [down_a, down_b], f32)
    rounds.leave(grad_w_down)
    grad_w_down = grad_w_down.reshape(EXPERTS, fs, d)
    rounds.turn()
    (qkv_slots,) = qkv_gather.finish()
    grads = []
    for slots in back_slots:
        g = join(along.slot_of, [slots], f32)
        if sub > 1:
            g = g.reshape(EXPERTS, sub, dl, n, fc)
            g = jnp.transpose(g, (0, 2, 3, 1, 4))
        grads.append(g.reshape(EXPERTS, dl, ff))
    grad_w_gate, grad_w_up = grads
    grad_w_out = join(along.slot_of, [out_slots], f32).reshape(dl, d)
    grad_w_query, grad_w_key, grad_w_value = columns(
        along.slot_of, *qkv_slots, (query_columns, key_columns, key_columns)
    )
    return (
        output,
        input_grad,
        small_grads[0],
        grad_w_query,
        grad_w_key,
        grad_w_value,
        grad_w_out,
        small_grads[1],
        small_grads[2:].T,
        grad_w_gate,
        grad_w_up,
        grad_w_down,
    )


def solution(mesh):
    seq = P("dp", "cp", None)
    row, mid = P("cp", None), P(None, "cp", None)
    in_specs = (seq, seq, seq, P("cp"), row, row, row, row, P("cp"), row, mid, mid, mid)
    out_specs = (seq, seq, P("cp"), row, row, row, row, P("cp"), row, mid, mid, mid)
    return jax.shard_map(local, mesh=mesh, in_specs=in_specs, out_specs=out_specs, check_vma=False)
```

```python
import functools
import math

import jax
import jax.numpy as jnp
from jax import lax
from jax.experimental import pallas as pl
from jax.experimental.pallas import tpu as pltpu
from jax.sharding import PartitionSpec as P

MODEL_WIDTH = 1536
QUERY_HEADS = 12
KEY_VALUE_HEADS = 2
HEAD_WIDTH = 128
EXPERTS = 8
TOPK = 4
BLK = 256

norm_eps = 1e-06
rope_base = 1000000.0
mask_fill = -1e30
score_scale = 1.0 / math.sqrt(HEAD_WIDTH)
query_columns = QUERY_HEADS * HEAD_WIDTH
key_columns = KEY_VALUE_HEADS * HEAD_WIDTH
group_heads = QUERY_HEADS // KEY_VALUE_HEADS

COST = 100000
EXTRA = 16
f32 = jnp.float32
bf16 = jnp.bfloat16


def dot_nn(a, b):
    return lax.dot_general(a, b, (((1,), (0,)), ((), ())), preferred_element_type=f32)


def dot_nt(a, b):
    return lax.dot_general(a, b, (((1,), (1,)), ((), ())), preferred_element_type=f32)


def dot_tn(a, b):
    return lax.dot_general(a, b, (((0,), (0,)), ((), ())), preferred_element_type=f32)


def params(megabytes):
    return pltpu.CompilerParams(vmem_limit_bytes=megabytes * 1024 * 1024)


def cost(flops, moved, raised=0):
    return pl.CostEstimate(flops=flops // COST, bytes_accessed=moved // COST, transcendentals=raised // COST)


def after(x, *deps):
    return lax.optimization_barrier((x, deps))[0]


def project_kernel(chunk_heads, half, slot_ref, h_ref, an_ref, af_ref, bn_ref, bf_ref, cos_ref, sin_ref, out_ref):
    j = pl.program_id(0)
    near = slot_ref[j] < half
    cut = an_ref.shape[1]

    def run(a_ref, b_ref):
        full = dot_nn(h_ref[:, :cut], a_ref[0]) + dot_nn(h_ref[:, cut:], b_ref[0])
        for k in range(chunk_heads):
            at = slice(k * HEAD_WIDTH, (k + 1) * HEAD_WIDTH)
            u = full[:, at]
            turned = u * cos_ref[...] + pltpu.roll(u, HEAD_WIDTH // 2, 1) * sin_ref[...]
            is_value = j * chunk_heads + k >= QUERY_HEADS + KEY_VALUE_HEADS
            out_ref[:, at] = jnp.where(is_value, u, turned).astype(bf16)

    pl.when(near)(lambda: run(an_ref, bn_ref))
    pl.when(jnp.logical_not(near))(lambda: run(af_ref, bf_ref))


def project(slot_of, h, w_a, w_b, cos, sin):
    half, cut, cw = w_a[0].shape
    t, d = h.shape
    m = 2 * half
    w_spec = pl.BlockSpec((1, cut, cw), lambda j, s: (s[j] % half, 0, 0))
    table = pl.BlockSpec((t, HEAD_WIDTH), lambda j, s: (0, 0))
    return pl.pallas_call(
        functools.partial(project_kernel, cw // HEAD_WIDTH, half),
        grid_spec=pltpu.PrefetchScalarGridSpec(
            num_scalar_prefetch=1,
            grid=(m,),
            in_specs=[pl.BlockSpec((t, d), lambda j, s: (0, 0))] + [w_spec] * 4 + [table] * 2,
            out_specs=pl.BlockSpec((t, cw), lambda j, s: (0, j)),
        ),
        out_shape=jax.ShapeDtypeStruct((t, m * cw), bf16),
        compiler_params=params(24),
        cost_estimate=cost(2 * t * d * m * cw, 2 * d * m * cw),
        name="project",
    )(slot_of, h, *w_a, *w_b, cos, sin)


def project_back_kernel(half, chunk_ref, h_ref, g_ref, an_ref, af_ref, bn_ref, bf_ref, dh_ref, gn_ref, gf_ref):
    j = pl.program_id(0)
    cut = an_ref.shape[1]

    @pl.when(j == 0)
    def _():
        dh_ref[...] = jnp.zeros_like(dh_ref)

    def run(a_ref, b_ref, gw_ref):
        dh_ref[:, :cut] += dot_nt(g_ref[...], a_ref[0])
        dh_ref[:, cut:] += dot_nt(g_ref[...], b_ref[0])
        gw_ref[0] = dot_tn(h_ref[...], g_ref[...]).astype(bf16)

    pl.when(j < half)(lambda: run(af_ref, bf_ref, gf_ref))
    pl.when(j >= half)(lambda: run(an_ref, bn_ref, gn_ref))


def project_back(chunk_of, h, grad, w_a, w_b):
    half, cut, cw = w_a[0].shape
    t, d = h.shape
    m = 2 * half
    first = lambda j, c: (jnp.minimum(j, half - 1), 0, 0)
    second = lambda j, c: (jnp.maximum(j - half, 0), 0, 0)
    near, far = pl.BlockSpec((1, cut, cw), second), pl.BlockSpec((1, cut, cw), first)
    return pl.pallas_call(
        functools.partial(project_back_kernel, half),
        grid_spec=pltpu.PrefetchScalarGridSpec(
            num_scalar_prefetch=1,
            grid=(m,),
            in_specs=[
                pl.BlockSpec((t, d), lambda j, c: (0, 0)),
                pl.BlockSpec((t, cw), lambda j, c: (0, c[(j + half) % m])),
                near,
                far,
                near,
                far,
            ],
            out_specs=[
                pl.BlockSpec((t, d), lambda j, c: (0, 0)),
                pl.BlockSpec((1, d, cw), second),
                pl.BlockSpec((1, d, cw), first),
            ],
        ),
        out_shape=[
            jax.ShapeDtypeStruct((t, d), f32),
            jax.ShapeDtypeStruct((half, d, cw), bf16),
            jax.ShapeDtypeStruct((half, d, cw), bf16),
        ],
        compiler_params=params(32),
        cost_estimate=cost(4 * t * d * m * cw, 4 * d * m * cw),
        name="project_back",
    )(chunk_of, h, grad, *w_a, *w_b)


def visible(rank, shape, dim):
    slot = lax.shift_right_logical(lax.broadcasted_iota(jnp.int32, shape, dim), BLK.bit_length() - 1)
    return (slot ^ rank) <= rank


def attend_kernel(rank_ref, q_ref, k_ref, v_ref, out_ref):
    s = dot_nt(q_ref[...], k_ref[...]) * score_scale
    s = jnp.where(visible(rank_ref[0], s.shape, 1), s, mask_fill)
    e = jnp.exp(s - jnp.max(s, 1, keepdims=True))
    p = (e / jnp.sum(e, 1, keepdims=True)).astype(bf16)
    out_ref[...] = dot_nn(p, v_ref[...]).astype(bf16)


def attend(rank, qkv, kv):
    t, rows = qkv.shape[0], kv.shape[0]
    return pl.pallas_call(
        attend_kernel,
        grid_spec=pltpu.PrefetchScalarGridSpec(
            num_scalar_prefetch=1,
            grid=(QUERY_HEADS,),
            in_specs=[
                pl.BlockSpec((t, HEAD_WIDTH), lambda j, s: (0, j)),
                pl.BlockSpec((rows, HEAD_WIDTH), lambda j, s: (0, j // group_heads)),
                pl.BlockSpec((rows, HEAD_WIDTH), lambda j, s: (0, KEY_VALUE_HEADS + j // group_heads)),
            ],
            out_specs=pl.BlockSpec((t, HEAD_WIDTH), lambda j, s: (0, j)),
        ),
        out_shape=jax.ShapeDtypeStruct((t, query_columns), bf16),
        compiler_params=params(40),
        cost_estimate=cost(4 * t * rows * query_columns, 4 * t * query_columns, t * rows * QUERY_HEADS),
        name="attend",
    )(rank, qkv, kv, kv)


def attend_back_kernel(rank_ref, q_ref, k_ref, v_ref, g_ref, cos_ref, sin_ref, dq_ref, dkv_ref, dk_acc, dv_acc):
    j = pl.program_id(0)
    q, k, g = q_ref[...], k_ref[...], g_ref[...]
    s = dot_nt(k, q) * score_scale
    s = jnp.where(visible(rank_ref[0], s.shape, 0), s, mask_fill)
    e = jnp.exp(s - jnp.max(s, 0, keepdims=True))
    p = e / jnp.sum(e, 0, keepdims=True)
    pb = p.astype(bf16)
    dp = dot_nt(v_ref[...], g)
    delta = jnp.sum(p * dp, 0, keepdims=True)
    ds = (p * (dp - delta)).astype(bf16)
    dq = dot_tn(ds, k) * score_scale
    dq_ref[...] = (dq * cos_ref[...] - pltpu.roll(dq, HEAD_WIDTH // 2, 1) * sin_ref[...]).astype(bf16)

    @pl.when(j % group_heads == 0)
    def _():
        dk_acc[...] = jnp.zeros_like(dk_acc)
        dv_acc[...] = jnp.zeros_like(dv_acc)

    dk_acc[...] += dot_nn(ds, q) * score_scale
    dv_acc[...] += dot_nn(pb, g)

    @pl.when(j % group_heads == group_heads - 1)
    def _():
        dkv_ref[0] = dk_acc[...].astype(bf16)
        dkv_ref[1] = dv_acc[...].astype(bf16)


def attend_back(rank, qkv, kv, grad, cos, sin):
    t, rows = qkv.shape[0], kv.shape[0]
    return pl.pallas_call(
        attend_back_kernel,
        grid_spec=pltpu.PrefetchScalarGridSpec(
            num_scalar_prefetch=1,
            grid=(QUERY_HEADS,),
            in_specs=[
                pl.BlockSpec((t, HEAD_WIDTH), lambda j, s: (0, j)),
                pl.BlockSpec((rows, HEAD_WIDTH), lambda j, s: (0, j // group_heads)),
                pl.BlockSpec((rows, HEAD_WIDTH), lambda j, s: (0, KEY_VALUE_HEADS + j // group_heads)),
                pl.BlockSpec((t, HEAD_WIDTH), lambda j, s: (0, j)),
                pl.BlockSpec((t, HEAD_WIDTH), lambda j, s: (0, 0)),
                pl.BlockSpec((t, HEAD_WIDTH), lambda j, s: (0, 0)),
            ],
            out_specs=[
                pl.BlockSpec((t, HEAD_WIDTH), lambda j, s: (0, j)),
                pl.BlockSpec((2, rows, HEAD_WIDTH), lambda j, s: (0, 0, j // group_heads)),
            ],
            scratch_shapes=[pltpu.VMEM((rows, HEAD_WIDTH), f32)] * 2,
        ),
        out_shape=[
            jax.ShapeDtypeStruct((t, query_columns), bf16),
            jax.ShapeDtypeStruct((2, rows, key_columns), bf16),
        ],
        compiler_params=params(56),
        cost_estimate=cost(10 * t * rows * query_columns, 8 * t * query_columns, t * rows * QUERY_HEADS),
        name="attend_back",
    )(rank, qkv, kv, kv, grad, cos, sin)


def experts_kernel(
    chunk_ref, h_ref, z_ref, gn_ref, gf_ref, un_ref, uf_ref, wd_ref,
    a_ref, dg_ref, du_ref, eo_ref, dh_ref, weights, eo_acc, dh_acc, dgate_acc, sems,
):
    per, fc, d = weights.shape[2:]
    ct = per * fc

    def copies(side):
        moves = [
            pltpu.make_async_copy((gn_ref, gf_ref)[side], weights.at[side, 0], sems.at[side, 0]),
            pltpu.make_async_copy((un_ref, uf_ref)[side], weights.at[side, 1], sems.at[side, 1]),
        ]
        for k in range(per):
            moves.append(
                pltpu.make_async_copy(
                    wd_ref.at[chunk_ref[side * per + k]], weights.at[side, 2, k], sems.at[side, 2 + k]
                )
            )
        return moves

    for side in range(2):
        for move in copies(side):
            move.start()
    t = z_ref.shape[0]
    gates_high = h_ref[t:, :t]
    gates_low = h_ref[t:, t : 2 * t]
    for side in range(2):
        moves = copies(side)
        slot_row = lax.broadcasted_iota(jnp.int32, (EXTRA, ct), 0)
        slot_col = lax.broadcasted_iota(jnp.int32, (EXTRA, ct), 1) + side * ct
        low = slot_row * fc
        pick = jnp.where((slot_col >= low) & (slot_col < low + fc), 1.0, 0.0).astype(bf16)
        wide = dot_tn(gates_high, pick) + dot_tn(gates_low, pick)
        moves[0].wait()
        wg = weights[side, 0].reshape(ct, d)
        g = dot_nt(h_ref[:t], wg)
        moves[1].wait()
        wu = weights[side, 1].reshape(ct, d)
        u = dot_nt(h_ref[:t], wu)
        for move in moves[2:]:
            move.wait()
        wd = weights[side, 2].reshape(ct, d)
        e = dot_nt(z_ref[...], wd)
        sig = 1.0 / (1.0 + jnp.exp(-g))
        swish = g * sig
        a = swish * u
        da = e * wide
        at = slice(side * ct, (side + 1) * ct)
        ab = (a * wide).astype(bf16)
        dg = (da * u * (sig * (1.0 + g * (1.0 - sig)))).astype(bf16)
        du = (da * swish).astype(bf16)
        a_ref[:, at] = ab
        dg_ref[:, at] = dg
        du_ref[:, at] = du
        dgate = dot_nt(pick, (a * e).astype(bf16))
        if side == 0:
            dgate_acc[...] = dgate
            dh_acc[...] = dot_nn(dg, wg)
            dh_acc[...] += dot_nn(du, wu)
            eo_acc[...] = dot_nn(ab, wd)
        else:
            dgate = dgate_acc[...] + dgate
            high = dgate.astype(dh_ref.dtype)
            dh_ref[t:] = jnp.zeros((EXTRA, d), dh_ref.dtype)
            dh_ref[t:, :t] = high
            dh_ref[t:, t : 2 * t] = (dgate - high.astype(f32)).astype(dh_ref.dtype)
            dh_acc[...] += dot_nn(dg, wg)
            dh_ref[:t] = (dh_acc[...] + dot_nn(du, wu)).astype(dh_ref.dtype)
            eo_ref[...] = (eo_acc[...] + dot_nn(ab, wd)).astype(eo_ref.dtype)


def experts(chunk_of, h, z, wg, wu, wd, sent_type):
    t, d = z.shape
    per, fc = wg[0].shape[0], wg[0].shape[1]
    width = 2 * per * fc
    vmem, hbm = pl.BlockSpec(memory_space=pltpu.VMEM), pl.BlockSpec(memory_space=pl.ANY)
    return pl.pallas_call(
        experts_kernel,
        in_specs=[pl.BlockSpec(memory_space=pltpu.SMEM)] + [vmem] * 2 + [hbm] * 5,
        out_specs=[vmem] * 5,
        out_shape=[
            jax.ShapeDtypeStruct((t, width), bf16),
            jax.ShapeDtypeStruct((t, width), bf16),
            jax.ShapeDtypeStruct((t, width), bf16),
            jax.ShapeDtypeStruct((t, d), sent_type),
            jax.ShapeDtypeStruct((t + EXTRA, d), sent_type),
        ],
        scratch_shapes=[
            pltpu.VMEM((2, 3, per, fc, d), bf16),
            pltpu.VMEM((t, d), f32),
            pltpu.VMEM((t, d), f32),
            pltpu.VMEM((EXTRA, t), f32),
            pltpu.SemaphoreType.DMA((2, 2 + per)),
        ],
        compiler_params=params(48),
        cost_estimate=cost(12 * t * d * width, 6 * d * width),
        name="experts",
    )(chunk_of, h, z, *wg, *wu, wd)


def expert_grads_kernel(n, fc, pairs, *refs):
    out_ref = refs[-1]
    per = out_ref.shape[0]
    rights = refs[pairs * n : -1]
    for which in range(pairs):
        left, right = refs[which * n : (which + 1) * n], rights
        total = dot_tn(left[0][...], right[0][...])
        for s in range(1, n):
            total += dot_tn(left[s][...], right[s][...])
        out_ref[:, which] = total.astype(bf16).reshape(per, fc, total.shape[-1])


def expert_grads(side, fc, lefts, right):
    n = len(right)
    t, width = lefts[0][0].shape
    width = width // 2
    d = right[0].shape[1]
    ct = min(width, 384)
    per = ct // fc
    steps = width // ct
    tile = pl.BlockSpec((t, ct), lambda j: (0, side * steps + j))
    rows = pl.BlockSpec((t, d), lambda j: (0, 0))
    if width % HEAD_WIDTH:
        lefts = [[x[:, side * width : (side + 1) * width] for x in xs] for xs in lefts]
        tile = pl.BlockSpec((t, width), lambda j: (0, 0))
    pairs = len(lefts)
    flat = [x for xs in lefts for x in xs]
    return pl.pallas_call(
        functools.partial(expert_grads_kernel, n, fc, pairs),
        grid=(steps,),
        in_specs=[tile] * (pairs * n) + [rows] * n,
        out_specs=pl.BlockSpec((per, pairs, fc, d), lambda j: (j, 0, 0, 0)),
        out_shape=jax.ShapeDtypeStruct((width // fc, pairs, fc, d), bf16),
        compiler_params=params(58),
        cost_estimate=cost(2 * pairs * n * t * d * width, 2 * pairs * d * width),
        name="expert_grads",
    )(*flat, *right)


def join_kernel(half, slot_ref, *refs):
    out_ref = refs[-1]
    near = slot_ref[pl.program_id(0)] < half

    def run(side):
        at = 0
        for k in range(side, len(refs) - 1, 2):
            block = refs[k][0]
            rows = block.shape[0]
            if out_ref.ndim == 4:
                out_ref[at : at + rows, 0] = block.astype(out_ref.dtype)
            else:
                out_ref[0, at : at + rows] = block.astype(out_ref.dtype)
            at += rows

    pl.when(near)(lambda: run(0))
    pl.when(jnp.logical_not(near))(lambda: run(1))


def join(slot_of, parts, dtype, spread_out=False):
    half = parts[0][0].shape[0]
    m = 2 * half
    tail = parts[0][0].shape[2:]
    rows = sum(near.shape[1] for near, far in parts)
    zeros = (0,) * len(tail)
    specs, flat = [], []
    for pair in parts:
        for x in pair:
            specs.append(pl.BlockSpec((1,) + x.shape[1:], lambda j, s: (s[j] % half, 0) + zeros))
            flat.append(x)
    if spread_out:
        out_spec = pl.BlockSpec((rows, 1) + tail, lambda j, s: (0, j) + zeros)
        shape = (rows, m) + tail
    else:
        out_spec = pl.BlockSpec((1, rows) + tail, lambda j, s: (j, 0) + zeros)
        shape = (m, rows) + tail
    return pl.pallas_call(
        functools.partial(join_kernel, half),
        grid_spec=pltpu.PrefetchScalarGridSpec(
            num_scalar_prefetch=1, grid=(m,), in_specs=specs, out_specs=out_spec
        ),
        out_shape=jax.ShapeDtypeStruct(shape, dtype),
        compiler_params=params(24),
        cost_estimate=cost(0, 6 * math.prod(shape)),
        name="join",
    )(slot_of, *flat)


def columns_kernel(half, counts, slot_ref, near_ref, far_ref, *out_refs):
    j = pl.program_id(0)
    near = slot_ref[j] < half
    at = 0
    for count, out_ref in zip(counts, out_refs):
        mine = (j >= at) & (j < at + count)

        @pl.when(mine & near)
        def _(out_ref=out_ref):
            out_ref[...] = near_ref[0].astype(f32)

        @pl.when(mine & jnp.logical_not(near))
        def _(out_ref=out_ref):
            out_ref[...] = far_ref[0].astype(f32)

        at += count


def columns(slot_of, near, far, widths):
    half, rows, cw = near.shape
    counts = [w // cw for w in widths]
    specs, at = [], 0
    for count in counts:
        specs.append(
            pl.BlockSpec((rows, cw), lambda j, s, at=at, top=count - 1: (0, jnp.clip(j - at, 0, top)))
        )
        at += count
    in_spec = pl.BlockSpec((1, rows, cw), lambda j, s: (s[j] % half, 0, 0))
    return pl.pallas_call(
        functools.partial(columns_kernel, half, counts),
        grid_spec=pltpu.PrefetchScalarGridSpec(
            num_scalar_prefetch=1, grid=(2 * half,), in_specs=[in_spec] * 2, out_specs=specs
        ),
        out_shape=[jax.ShapeDtypeStruct((rows, w), f32) for w in widths],
        compiler_params=params(16),
        cost_estimate=cost(0, 12 * near.size),
        name="columns",
    )(slot_of, near, far)


def arrange_kernel(n, fc, rank_ref, *refs):
    slots, (gate_ref, up_ref) = refs[:n], refs[n:]
    dl = slots[0].shape[1]

    def run(rank):
        for q in range(n):
            block = slots[q ^ rank]
            gate_ref[:, q * dl : (q + 1) * dl] = block[:fc]
            up_ref[:, q * dl : (q + 1) * dl] = block[fc : 2 * fc]

    for rank in range(n):
        pl.when(rank_ref[0] == rank)(functools.partial(run, rank))


def arrange(rank, slots, fc):
    n, d = len(slots), len(slots) * slots[0].shape[1]
    vmem = pl.BlockSpec(memory_space=pltpu.VMEM)
    return pl.pallas_call(
        functools.partial(arrange_kernel, n, fc),
        in_specs=[pl.BlockSpec(memory_space=pltpu.SMEM)] + [vmem] * n,
        out_specs=[vmem] * 2,
        out_shape=[jax.ShapeDtypeStruct((fc, d), bf16)] * 2,
        compiler_params=params(16),
        cost_estimate=cost(0, 8 * fc * d),
        name="arrange",
    )(rank, *slots)


def turn_back_kernel(n, fc, rank_ref, *refs):
    slots, out_ref, rows = refs[:n], refs[n], refs[n + 1]

    def run(rank):
        for k in range(2):
            for q in range(n):
                rows[k, q * fc : (q + 1) * fc] = slots[q ^ rank][k * fc : (k + 1) * fc].astype(f32)

    for rank in range(n):
        pl.when(rank_ref[0] == rank)(functools.partial(run, rank))
    for k in range(2):
        out_ref[k] = rows[k].T.astype(bf16)


def turn_back(rank, slots, fc):
    n, dl = len(slots), slots[0].shape[1]
    if fc % 16 or dl % HEAD_WIDTH or n * fc % HEAD_WIDTH:
        stacked = jnp.stack(slots).reshape(n, 2, fc, dl)
        stacked = jnp.take(stacked, jnp.arange(n) ^ rank, axis=0)
        return jnp.transpose(stacked, (1, 3, 0, 2)).reshape(2, dl, n * fc)
    vmem = pl.BlockSpec(memory_space=pltpu.VMEM)
    return pl.pallas_call(
        functools.partial(turn_back_kernel, n, fc),
        in_specs=[pl.BlockSpec(memory_space=pltpu.SMEM)] + [vmem] * n,
        out_specs=vmem,
        out_shape=jax.ShapeDtypeStruct((2, dl, n * fc), bf16),
        scratch_shapes=[pltpu.VMEM((2, n * fc, dl), f32)],
        compiler_params=params(24),
        cost_estimate=cost(0, 8 * n * fc * dl),
        name="turn_back",
    )(rank, *slots)


class Rounds:
    def __init__(self):
        self.gate, self.made, self.later = (), [], []

    def enter(self, x):
        return after(x, *self.gate) if self.gate else x

    def leave(self, *xs):
        self.made.extend(xs)
        return xs[0]

    def leave_late(self, *xs):
        self.later.extend(xs)
        return xs[0]

    def turn(self):
        self.gate, self.made, self.later = tuple(self.made), self.later, []


class Along:
    def __init__(self, rounds):
        self.rounds = rounds
        self.n, self.m = lax.axis_size("cp"), lax.axis_size("dp")
        self.r, self.i = lax.axis_index("cp"), lax.axis_index("dp")
        self.bits = self.m.bit_length() - 1
        assert 1 << self.bits == self.m and self.bits > 1
        self.inner = self.bits - 1
        slots = jnp.arange(self.m, dtype=jnp.int32)
        self.chunk_of = self.i ^ (((slots & (self.m // 2 - 1)) << 1) | (slots >> self.inner))
        offset = slots ^ self.i
        self.slot_of = (offset >> 1) | ((offset & 1) << self.inner)

    def send(self, x, axis, pairs, late=False):
        leave = self.rounds.leave_late if late else self.rounds.leave
        return leave(lax.ppermute(self.rounds.enter(x), axis, pairs))

    def swap(self, x, bit, late=False):
        mask = 1 if bit == self.inner else 2 << bit
        return self.send(x, "dp", [(k, k ^ mask) for k in range(self.m)], late)

    def cross(self, x, s, keep=None, late=False):
        pairs = [(k, k ^ s) for k in range(self.n)]
        return self.send(x, "cp", [p for p in pairs if keep is None or keep(*p)], late)

    def orders(self):
        up = list(range(self.inner))
        return up, up[::-1]

    def pieces(self, x, s):
        return lax.dynamic_index_in_dim(x, self.r ^ s, 0, keepdims=False)

    def scatter_cp(self, x):
        return [self.pieces(x, 0)] + [self.cross(self.pieces(x, s), s) for s in range(1, self.n)]

    def ranked(self, slots):
        for bit in range(self.n.bit_length() - 1):
            turned = (self.r >> bit & 1) == 1
            slots = [jnp.where(turned, slots[k ^ 1 << bit], slots[k]) for k in range(self.n)]
        return jnp.stack(slots)

    def gather_cp(self, x):
        return [x] + [self.cross(x, s) for s in range(1, self.n)]


class Gather:
    def __init__(self, along, *xs):
        self.along, self.parts, self.at = along, [{0: x} for x in xs], 0

    def step(self, late=False):
        for k, held in enumerate(self.parts):
            bit = self.along.orders()[k % 2][self.at]
            slots = sorted(held)
            got = self.along.swap(jnp.stack([held[h] for h in slots]), bit, late)
            for p, h in enumerate(slots):
                held[h | 1 << bit] = got[p]
        self.at += 1

    def rest(self, late=False):
        while self.at < self.along.inner:
            self.step(late)

    def finish(self, late=False):
        self.rest(late)
        near = [jnp.stack([held[h] for h in sorted(held)]) for held in self.parts]
        return [(x, self.along.swap(x, self.along.inner, late)) for x in near]


class Reduce:
    def __init__(self, along, far):
        self.along, self.at = along, 0
        self.got = along.swap(far, along.inner)

    def add(self, near):
        cut = near.shape[1] // 2
        self.parts = [
            {h: near[h, at].astype(f32) + self.got[h, at].astype(f32) for h in range(self.along.m // 2)}
            for at in (slice(0, cut), slice(cut, None))
        ]

    def step(self, late=False):
        for k, held in enumerate(self.parts):
            bit = self.along.orders()[1 - k][self.at]
            sent = jnp.stack([held[h].astype(bf16) for h in sorted(held) if h >> bit & 1])
            more = self.along.swap(sent, bit, late)
            kept = [h for h in sorted(held) if not h >> bit & 1]
            self.parts[k] = {h: held[h] + more[p].astype(f32) for p, h in enumerate(kept)}
        self.at += 1

    def rest(self, late=False):
        while self.at < self.along.inner:
            self.step(late)

    def finish(self):
        self.rest()
        return jnp.concatenate([p[0] for p in self.parts], 0).astype(bf16)


class Relay:
    inside, outside, turned = [(1, 2), (2, 1)], [(1, 0), (2, 3)], [(0, 1), (3, 2)]

    def __init__(self, along, x):
        self.along, self.x, self.four = along, x, along.n == 4

    def one(self):
        self.first = self.along.cross(self.x, 1)

    def middle(self):
        if self.four:
            self.third = self.along.send(self.x, "cp", self.inside)

    def two(self, late=False):
        self.second = self.along.cross(self.x, 2, late=late)

    def ends(self):
        along = self.along
        if self.four:
            outer = along.send(self.second, "cp", self.outside)
            self.third = [jnp.where((along.r == 1) | (along.r == 2), self.third, outer)]
        else:
            self.third = [along.cross(self.x, s) for s in range(3, along.n)]

    def slots(self):
        return [self.x, self.first, self.second, *self.third]


def norm_forward(values, gain_vec):
    inverse = lax.rsqrt(jnp.mean(values * values, -1, keepdims=True) + norm_eps)
    scaled = values * inverse
    return (scaled * gain_vec, scaled, inverse)


def norm_backward(gradient, gain_vec, scaled, inverse):
    gain_grad = jnp.sum(gradient * scaled, 0)
    inner_vals = gradient * gain_vec
    return (
        inverse * (inner_vals - scaled * jnp.mean(inner_vals * scaled, -1, keepdims=True)),
        gain_grad,
    )


def rotary(positions):
    half = HEAD_WIDTH // 2
    frequency = rope_base ** (-2.0 * jnp.arange(half, dtype=f32) / HEAD_WIDTH)
    angles = positions.astype(f32)[:, None] * frequency[None, :]
    cos, sin = jnp.cos(angles), jnp.sin(angles)
    return jnp.concatenate([cos, cos], 1), jnp.concatenate([-sin, sin], 1)


def local(
    tokens, routes, out_grad, norm_attn, w_query, key_weight, value_weight, w_out,
    norm_mix, w_router, w_gate, w_up, w_down,
):
    rounds = Rounds()
    along = Along(rounds)
    n, m, r, i = along.n, along.m, along.r, along.i
    t, d = tokens.shape[1], tokens.shape[2]
    assert t == BLK
    dl, ff, fs = w_query.shape[0], w_gate.shape[2], w_down.shape[1]
    sub = m // EXPERTS
    fc = fs // sub
    rc = dl // m
    inputs = tokens[0].astype(f32)
    route_rows = routes[0]
    dz = out_grad[0]
    up = lambda a, b: b > a
    down = lambda a, b: b < a

    w_qkv = jnp.concatenate([w_query, key_weight, value_weight], 1)
    cw = w_qkv.shape[1] // m
    small = jnp.concatenate([norm_attn[None], norm_mix[None], w_router.T], 0).reshape(-1)
    tail = -(-small.shape[0] // (16 * cw)) * 16
    small = jnp.concatenate([small, jnp.zeros((tail * cw - small.shape[0],), bf16)]).reshape(tail, cw)
    sent = jnp.concatenate([lax.dynamic_slice_in_dim(w_qkv, i * cw, cw, 1), small], 0)
    got = along.ranked(along.gather_cp(sent))
    own_qkv = got[:, :dl].reshape(d, cw)
    small = got[:, dl:].reshape(n, tail * cw)[:, : (2 + EXPERTS) * dl].reshape(n, 2 + EXPERTS, dl)
    small = jnp.swapaxes(small, 0, 1).reshape(2 + EXPERTS, d)
    gain_one, gain_two = small[0].astype(f32), small[1].astype(f32)
    router = small[2:]
    flipped = [
        lax.dynamic_index_in_dim(w, i // sub, 0, keepdims=False).T.reshape(n, sub, fc, dl)
        for w in (w_gate, w_up)
    ]
    flipped = lax.dynamic_index_in_dim(jnp.stack(flipped, 1), i % sub, 2, keepdims=False).reshape(n, 2 * fc, dl)
    flipped = rounds.leave(flipped)
    out_rows = lax.dynamic_slice_in_dim(w_out, i * rc, rc, 0)
    cos, sin = rotary(r * t + jnp.arange(t, dtype=jnp.int32))
    rounds.leave(cos, sin)

    rounds.turn()
    qkv_gather = Gather(along, own_qkv[: d // 2], own_qkv[d // 2 :])
    qkv_gather.step()
    own_out = along.gather_cp(out_rows)
    normed_one, scaled_one, inverse_one = norm_forward(inputs, gain_one)
    h1 = rounds.leave(normed_one.astype(bf16))
    rounds.turn()
    qkv_gather.rest()
    mix = [along.pieces(flipped, 0)] + [along.cross(along.pieces(flipped, s), s) for s in (1, 2)]
    own_out = rounds.leave(along.ranked(own_out))
    rounds.turn()
    qkv_a, qkv_b = qkv_gather.finish()
    mix.extend(along.cross(along.pieces(flipped, s), s, late=True) for s in range(3, n))
    rounds.turn()
    rank = r.reshape(1)
    out_gather = Gather(along, own_out[: n // 2], own_out[n // 2 :])
    out_gather.step()
    qkv = rounds.leave(project(along.slot_of, rounds.enter(h1), qkv_a, qkv_b, cos, sin))
    rounds.turn()

    own_kv = qkv[:, query_columns:]
    kv = jnp.concatenate([own_kv] + [along.cross(own_kv, s, up) for s in range(1, n)], 0)
    out_gather.rest()
    if dl % HEAD_WIDTH == 0:
        gate_rows, up_rows = arrange(rank, [rounds.enter(x) for x in mix], fc)
    else:
        gate_rows, up_rows = jnp.swapaxes(along.ranked(mix), 0, 1).reshape(2, fc, d)
    mix_gather = Gather(along, gate_rows, up_rows)
    mix_gather.step()
    rounds.turn()
    z_relay = Relay(along, dz)
    z_relay.two()
    mix_gather.rest()
    out_a, out_b = out_gather.finish()
    ob = rounds.leave(attend(rank, qkv, rounds.enter(kv)))
    full_out = join(along.slot_of, [out_a, out_b], bf16, True).reshape(n * dl, d)
    full_out = rounds.leave(full_out)
    rounds.turn()
    z_relay.one()
    z_relay.middle()
    wg, wu = mix_gather.finish()
    wd = w_down.reshape(m, fc, d)

    middle = inputs + dot_nn(rounds.enter(ob), full_out)
    normed_two, scaled_two, inverse_two = norm_forward(middle, gain_two)
    h2 = normed_two.astype(bf16)
    logits = dot_nt(h2, router)
    experts_range = jnp.arange(EXPERTS, dtype=jnp.int32)
    route_flags = (route_rows[:, :, None] == experts_range).astype(f32)
    chosen = jnp.sum(logits[:, None, :] * route_flags, -1)
    raised = jnp.exp(chosen - jnp.max(chosen, -1, keepdims=True))
    gate_vals = raised / jnp.sum(raised, -1, keepdims=True)
    slot_flags = (route_rows[:, :, None] == along.chunk_of // sub).astype(f32)
    gates = jnp.sum(gate_vals[:, :, None] * slot_flags, 1).T
    gates = jnp.concatenate([gates, jnp.zeros((EXTRA - m, t), f32)], 0)
    gates_high = gates.astype(bf16)
    gates_low = (gates - gates_high.astype(f32)).astype(bf16)
    gates = jnp.concatenate([gates_high, gates_low, jnp.zeros((EXTRA, d - 2 * t), bf16)], 1)
    h_sent = rounds.leave(jnp.concatenate([h2, gates], 0))
    rounds.turn()

    h_relay = Relay(along, h_sent)
    h_relay.one()
    h_relay.middle()

    def run(h, z, sent_type=bf16):
        results = experts(along.chunk_of, rounds.enter(h), z, wg, wu, wd, sent_type)
        rounds.leave(*results)
        return results

    done = [run(h_sent, dz, f32)]
    rounds.turn()
    h_relay.two()
    z_relay.ends()
    done.append(run(h_relay.first, z_relay.first))
    rounds.turn()
    h_relay.ends()
    done.append(run(h_relay.second, z_relay.second))
    rounds.turn()
    h_slots, z_slots = h_relay.slots(), z_relay.slots()
    h2_back = done[0][4] + along.cross(done[1][4], 1).astype(f32)
    done.extend(run(h_slots[s], z_slots[s]) for s in range(3, n))
    rounds.turn()
    triples = [[rounds.enter(x[k]) for x in done] for k in range(3)]
    second = done[2][4]
    if n == 4:
        h2_back = h2_back + along.send(done[3][4], "cp", Relay.inside).astype(f32)
        second = (second.astype(f32) + along.send(done[3][4], "cp", Relay.turned).astype(f32)).astype(bf16)
    else:
        for s in range(3, n):
            h2_back = h2_back + along.cross(done[s][4], s).astype(f32)
    mix_far = rounds.leave(expert_grads(1, fc, triples[1:], h_slots).reshape(m // 2, 2 * fc, d))
    mix_reduce = Reduce(along, mix_far)
    mix_near = rounds.leave(expert_grads(0, fc, triples[1:], h_slots).reshape(m // 2, 2 * fc, d))
    rounds.turn()
    h2_back = h2_back + along.cross(second, 2).astype(f32)
    mix_reduce.add(mix_near)
    mix_reduce.rest()
    acts = [rounds.enter(x) for x in triples[0]]
    down_grads = [expert_grads(side, fc, [acts], z_slots).reshape(m // 2, fc, d) for side in (0, 1)]
    down_grads = rounds.leave(join(along.slot_of, [down_grads], bf16))
    rounds.turn()
    own_mix = mix_reduce.finish()
    back = [lax.dynamic_slice_in_dim(own_mix, (r ^ s) * dl, dl, 1) for s in range(n)]
    back = [back[0]] + [along.cross(back[s], s) for s in range(1, n)]
    mixed = done[0][3] + along.cross(done[1][3], 1).astype(f32)
    h2_back = rounds.enter(h2_back)
    slot_gate_grad = h2_back[t : t + m, :t] + h2_back[t : t + m, t : 2 * t]
    gate_grad = jnp.sum(slot_gate_grad.T[:, None, :] * slot_flags, -1)
    weighted = gate_vals * gate_grad
    chosen_grad = weighted - gate_vals * jnp.sum(weighted, -1, keepdims=True)
    logit_grad = jnp.sum(chosen_grad[:, :, None] * route_flags, 1).astype(bf16)
    router_grad = dot_tn(logit_grad, h2)
    h2_grad = h2_back[:t] + dot_nn(logit_grad, router)
    middle_norm_grad, gain_two_grad = norm_backward(h2_grad, gain_two, scaled_two, inverse_two)
    middle_grad = dz.astype(f32) + middle_norm_grad
    branch = middle_grad.astype(bf16)

    dob = dot_nt(branch, full_out).astype(bf16)
    out_grads = jnp.swapaxes(dot_tn(ob, branch).astype(bf16).reshape(n, m, rc, d), 0, 1).reshape(m * n * rc, d)
    out_grads = lax.psum_scatter(out_grads, "dp", scatter_dimension=0, tiled=True)
    dq, dkv = attend_back(rank, qkv, kv, dob, cos, sin)
    rounds.leave(dkv)
    rounds.turn()
    dkv_own = dkv[:, :t].astype(f32)
    for s in range(1, n):
        dkv_own = dkv_own + along.cross(dkv[:, s * t : (s + 1) * t], s, down).astype(f32)
    back = turn_back(rank, [rounds.enter(x) for x in back], fc)
    back_gather = Gather(along, back[0], back[1])
    back_gather.step()
    rounds.turn()
    back_gather.rest()
    down_grads = lax.psum(rounds.enter(after(down_grads, out_grads)), "dp")
    grad_w_down = down_grads.reshape(EXPERTS, fs, d).astype(f32)
    second_out = done[2][3]
    if n == 4:
        mixed = mixed + along.send(done[3][3], "cp", Relay.inside).astype(f32)
        second_out = second_out.astype(f32) + along.send(done[3][3], "cp", Relay.turned).astype(f32)
        second_out = second_out.astype(bf16)
    dkv_own = rounds.enter(dkv_own)
    dk = dkv_own[0].reshape(t, KEY_VALUE_HEADS, HEAD_WIDTH)
    half = HEAD_WIDTH // 2
    dk = dk * cos[:, None] - jnp.concatenate([dk[..., half:], dk[..., :half]], -1) * sin[:, None]
    dqkv = jnp.concatenate([dq, dk.reshape(t, key_columns).astype(bf16), dkv_own[1].astype(bf16)], 1)
    h1_grad, qkv_near, qkv_far = project_back(along.chunk_of, h1, dqkv, qkv_a, qkv_b)
    rounds.leave(h1_grad, qkv_near, qkv_far)
    qkv_reduce = Reduce(along, qkv_far)
    rounds.turn()
    qkv_reduce.add(qkv_near)
    qkv_reduce.step()
    back_slots = back_gather.finish()
    out_grads = lax.all_to_all(rounds.enter(out_grads.reshape(n, rc, d)), "cp", 0, 0, tiled=True)
    out_grads = rounds.leave(jnp.sum(out_grads.astype(f32), 0).astype(bf16))
    input_norm_grad, gain_one_grad = norm_backward(rounds.enter(h1_grad), gain_one, scaled_one, inverse_one)
    input_grad = (middle_grad + input_norm_grad).astype(bf16)[None]
    small_grads = jnp.concatenate([gain_one_grad[None], gain_two_grad[None], router_grad], 0)
    rounds.leave(small_grads)
    rounds.turn()
    qkv_reduce.rest()
    small_grads = small_grads + along.swap(small_grads, along.inner)
    second_out = rounds.enter(second_out)
    mixed = mixed + lax.ppermute(second_out, "cp", [(k, k ^ 2) for k in range(n)]).astype(f32)
    grad_w_out = lax.all_gather(rounds.enter(out_grads), "dp", axis=0, tiled=True).astype(f32)
    grads = []
    for slots in back_slots:
        g = rounds.leave(join(along.slot_of, [[rounds.enter(x) for x in slots]], f32))
        if sub > 1:
            g = g.reshape(EXPERTS, sub, dl, n, fc)
            g = jnp.transpose(g, (0, 2, 3, 1, 4))
        grads.append(g.reshape(EXPERTS, dl, ff))
    grad_w_gate, grad_w_up = grads
    rounds.turn()
    own_qkv = qkv_reduce.finish().reshape(n, dl, cw)
    own_qkv = [along.pieces(own_qkv, 0)] + [along.cross(along.pieces(own_qkv, s), s) for s in range(1, n)]
    own_qkv = functools.reduce(jnp.add, [x.astype(f32) for x in own_qkv]).astype(bf16)
    small_grads = small_grads + along.swap(small_grads, 0)
    if n != 4:
        for s in range(3, n):
            mixed = mixed + along.cross(done[s][3], s).astype(f32)
    rounds.turn()
    qkv_gather = Gather(along, own_qkv)
    qkv_gather.step()
    for bit in range(1, along.inner):
        small_grads = small_grads + along.swap(small_grads, bit)
    rounds.turn()
    qkv_gather.rest()
    small_grads = small_grads + along.cross(small_grads, 1)
    rounds.turn()
    (qkv_slots,) = qkv_gather.finish()
    for bit in range(1, n.bit_length() - 1):
        small_grads = small_grads + along.cross(small_grads, 1 << bit)
    output = (middle + mixed).astype(bf16)[None]
    small_grads = lax.dynamic_index_in_dim(small_grads.reshape(2 + EXPERTS, n, dl), r, 1, keepdims=False)
    grad_w_query, grad_w_key, grad_w_value = columns(
        along.slot_of, *qkv_slots, (query_columns, key_columns, key_columns)
    )
    return (
        output,
        input_grad,
        small_grads[0],
        grad_w_query,
        grad_w_key,
        grad_w_value,
        grad_w_out,
        small_grads[1],
        small_grads[2:].T,
        grad_w_gate,
        grad_w_up,
        grad_w_down,
    )


def solution(mesh):
    seq = P("dp", "cp", None)
    row, mid = P("cp", None), P(None, "cp", None)
    in_specs = (seq, seq, seq, P("cp"), row, row, row, row, P("cp"), row, mid, mid, mid)
    out_specs = (seq, seq, P("cp"), row, row, row, row, P("cp"), row, mid, mid, mid)
    return jax.shard_map(local, mesh=mesh, in_specs=in_specs, out_specs=out_specs, check_vma=False)
```

```python
import functools
import math

import jax
import jax.numpy as jnp
from jax import lax
from jax.experimental import pallas as pl
from jax.experimental.pallas import tpu as pltpu
from jax.sharding import PartitionSpec as P

MODEL_WIDTH = 1536
QUERY_HEADS = 12
KEY_VALUE_HEADS = 2
HEAD_WIDTH = 128
EXPERTS = 8
TOPK = 4
BLK = 256

norm_eps = 1e-06
rope_base = 1000000.0
mask_fill = -1e30
score_scale = 1.0 / math.sqrt(HEAD_WIDTH)
query_columns = QUERY_HEADS * HEAD_WIDTH
key_columns = KEY_VALUE_HEADS * HEAD_WIDTH
group_heads = QUERY_HEADS // KEY_VALUE_HEADS

COST = 100000
EXTRA = 16
f32 = jnp.float32
bf16 = jnp.bfloat16


def dot_nn(a, b):
    return lax.dot_general(a, b, (((1,), (0,)), ((), ())), preferred_element_type=f32)


def dot_nt(a, b):
    return lax.dot_general(a, b, (((1,), (1,)), ((), ())), preferred_element_type=f32)


def dot_tn(a, b):
    return lax.dot_general(a, b, (((0,), (0,)), ((), ())), preferred_element_type=f32)


def params(megabytes):
    return pltpu.CompilerParams(vmem_limit_bytes=megabytes * 1024 * 1024)


def cost(flops, moved, raised=0):
    return pl.CostEstimate(flops=flops // COST, bytes_accessed=moved // COST, transcendentals=raised // COST)


def after(x, *deps):
    return lax.optimization_barrier((x, deps))[0]


def project_kernel(chunk_heads, half, slot_ref, h_ref, an_ref, af_ref, bn_ref, bf_ref, cos_ref, sin_ref, out_ref):
    j = pl.program_id(0)
    near = slot_ref[j] < half
    cut = an_ref.shape[1]

    def run(a_ref, b_ref):
        full = dot_nn(h_ref[:, :cut], a_ref[0]) + dot_nn(h_ref[:, cut:], b_ref[0])
        for k in range(chunk_heads):
            at = slice(k * HEAD_WIDTH, (k + 1) * HEAD_WIDTH)
            u = full[:, at]
            turned = u * cos_ref[...] + pltpu.roll(u, HEAD_WIDTH // 2, 1) * sin_ref[...]
            is_value = j * chunk_heads + k >= QUERY_HEADS + KEY_VALUE_HEADS
            out_ref[:, at] = jnp.where(is_value, u, turned).astype(bf16)

    pl.when(near)(lambda: run(an_ref, bn_ref))
    pl.when(jnp.logical_not(near))(lambda: run(af_ref, bf_ref))


def project(slot_of, h, w_a, w_b, cos, sin):
    half, cut, cw = w_a[0].shape
    t, d = h.shape
    m = 2 * half
    w_spec = pl.BlockSpec((1, cut, cw), lambda j, s: (s[j] % half, 0, 0))
    table = pl.BlockSpec((t, HEAD_WIDTH), lambda j, s: (0, 0))
    return pl.pallas_call(
        functools.partial(project_kernel, cw // HEAD_WIDTH, half),
        grid_spec=pltpu.PrefetchScalarGridSpec(
            num_scalar_prefetch=1,
            grid=(m,),
            in_specs=[pl.BlockSpec((t, d), lambda j, s: (0, 0))] + [w_spec] * 4 + [table] * 2,
            out_specs=pl.BlockSpec((t, cw), lambda j, s: (0, j)),
        ),
        out_shape=jax.ShapeDtypeStruct((t, m * cw), bf16),
        compiler_params=params(24),
        cost_estimate=cost(2 * t * d * m * cw, 2 * d * m * cw),
        name="project",
    )(slot_of, h, *w_a, *w_b, cos, sin)


def project_back_kernel(half, chunk_ref, h_ref, g_ref, an_ref, af_ref, bn_ref, bf_ref, dh_ref, gn_ref, gf_ref):
    j = pl.program_id(0)
    cut = an_ref.shape[1]

    @pl.when(j == 0)
    def _():
        dh_ref[...] = jnp.zeros_like(dh_ref)

    def run(a_ref, b_ref, gw_ref):
        dh_ref[:, :cut] += dot_nt(g_ref[...], a_ref[0])
        dh_ref[:, cut:] += dot_nt(g_ref[...], b_ref[0])
        gw_ref[0] = dot_tn(h_ref[...], g_ref[...]).astype(bf16)

    pl.when(j < half)(lambda: run(af_ref, bf_ref, gf_ref))
    pl.when(j >= half)(lambda: run(an_ref, bn_ref, gn_ref))


def project_back(chunk_of, h, grad, w_a, w_b):
    half, cut, cw = w_a[0].shape
    t, d = h.shape
    m = 2 * half
    first = lambda j, c: (jnp.minimum(j, half - 1), 0, 0)
    second = lambda j, c: (jnp.maximum(j - half, 0), 0, 0)
    near, far = pl.BlockSpec((1, cut, cw), second), pl.BlockSpec((1, cut, cw), first)
    return pl.pallas_call(
        functools.partial(project_back_kernel, half),
        grid_spec=pltpu.PrefetchScalarGridSpec(
            num_scalar_prefetch=1,
            grid=(m,),
            in_specs=[
                pl.BlockSpec((t, d), lambda j, c: (0, 0)),
                pl.BlockSpec((t, cw), lambda j, c: (0, c[(j + half) % m])),
                near,
                far,
                near,
                far,
            ],
            out_specs=[
                pl.BlockSpec((t, d), lambda j, c: (0, 0)),
                pl.BlockSpec((1, d, cw), second),
                pl.BlockSpec((1, d, cw), first),
            ],
        ),
        out_shape=[
            jax.ShapeDtypeStruct((t, d), f32),
            jax.ShapeDtypeStruct((half, d, cw), bf16),
            jax.ShapeDtypeStruct((half, d, cw), bf16),
        ],
        compiler_params=params(32),
        cost_estimate=cost(4 * t * d * m * cw, 4 * d * m * cw),
        name="project_back",
    )(chunk_of, h, grad, *w_a, *w_b)


def visible(rank, shape, dim):
    slot = lax.shift_right_logical(lax.broadcasted_iota(jnp.int32, shape, dim), BLK.bit_length() - 1)
    return (slot ^ rank) <= rank


def attend_kernel(rank_ref, q_ref, k_ref, v_ref, out_ref):
    s = dot_nt(q_ref[...], k_ref[...]) * score_scale
    s = jnp.where(visible(rank_ref[0], s.shape, 1), s, mask_fill)
    e = jnp.exp(s - jnp.max(s, 1, keepdims=True))
    p = (e / jnp.sum(e, 1, keepdims=True)).astype(bf16)
    out_ref[...] = dot_nn(p, v_ref[...]).astype(bf16)


def attend(rank, qkv, kv):
    t, rows = qkv.shape[0], kv.shape[0]
    return pl.pallas_call(
        attend_kernel,
        grid_spec=pltpu.PrefetchScalarGridSpec(
            num_scalar_prefetch=1,
            grid=(QUERY_HEADS,),
            in_specs=[
                pl.BlockSpec((t, HEAD_WIDTH), lambda j, s: (0, j)),
                pl.BlockSpec((rows, HEAD_WIDTH), lambda j, s: (0, j // group_heads)),
                pl.BlockSpec((rows, HEAD_WIDTH), lambda j, s: (0, KEY_VALUE_HEADS + j // group_heads)),
            ],
            out_specs=pl.BlockSpec((t, HEAD_WIDTH), lambda j, s: (0, j)),
        ),
        out_shape=jax.ShapeDtypeStruct((t, query_columns), bf16),
        compiler_params=params(40),
        cost_estimate=cost(4 * t * rows * query_columns, 4 * t * query_columns, t * rows * QUERY_HEADS),
        name="attend",
    )(rank, qkv, kv, kv)


def attend_back_kernel(rank_ref, q_ref, k_ref, v_ref, g_ref, cos_ref, sin_ref, dq_ref, dkv_ref, dk_acc, dv_acc):
    j = pl.program_id(0)
    q, k, g = q_ref[...], k_ref[...], g_ref[...]
    s = dot_nt(k, q) * score_scale
    s = jnp.where(visible(rank_ref[0], s.shape, 0), s, mask_fill)
    e = jnp.exp(s - jnp.max(s, 0, keepdims=True))
    p = e / jnp.sum(e, 0, keepdims=True)
    pb = p.astype(bf16)
    dp = dot_nt(v_ref[...], g)
    delta = jnp.sum(p * dp, 0, keepdims=True)
    ds = (p * (dp - delta)).astype(bf16)
    dq = dot_tn(ds, k) * score_scale
    dq_ref[...] = (dq * cos_ref[...] - pltpu.roll(dq, HEAD_WIDTH // 2, 1) * sin_ref[...]).astype(bf16)

    @pl.when(j % group_heads == 0)
    def _():
        dk_acc[...] = jnp.zeros_like(dk_acc)
        dv_acc[...] = jnp.zeros_like(dv_acc)

    dk_acc[...] += dot_nn(ds, q) * score_scale
    dv_acc[...] += dot_nn(pb, g)

    @pl.when(j % group_heads == group_heads - 1)
    def _():
        dkv_ref[0] = dk_acc[...].astype(bf16)
        dkv_ref[1] = dv_acc[...].astype(bf16)


def attend_back(rank, qkv, kv, grad, cos, sin):
    t, rows = qkv.shape[0], kv.shape[0]
    return pl.pallas_call(
        attend_back_kernel,
        grid_spec=pltpu.PrefetchScalarGridSpec(
            num_scalar_prefetch=1,
            grid=(QUERY_HEADS,),
            in_specs=[
                pl.BlockSpec((t, HEAD_WIDTH), lambda j, s: (0, j)),
                pl.BlockSpec((rows, HEAD_WIDTH), lambda j, s: (0, j // group_heads)),
                pl.BlockSpec((rows, HEAD_WIDTH), lambda j, s: (0, KEY_VALUE_HEADS + j // group_heads)),
                pl.BlockSpec((t, HEAD_WIDTH), lambda j, s: (0, j)),
                pl.BlockSpec((t, HEAD_WIDTH), lambda j, s: (0, 0)),
                pl.BlockSpec((t, HEAD_WIDTH), lambda j, s: (0, 0)),
            ],
            out_specs=[
                pl.BlockSpec((t, HEAD_WIDTH), lambda j, s: (0, j)),
                pl.BlockSpec((2, rows, HEAD_WIDTH), lambda j, s: (0, 0, j // group_heads)),
            ],
            scratch_shapes=[pltpu.VMEM((rows, HEAD_WIDTH), f32)] * 2,
        ),
        out_shape=[
            jax.ShapeDtypeStruct((t, query_columns), bf16),
            jax.ShapeDtypeStruct((2, rows, key_columns), bf16),
        ],
        compiler_params=params(56),
        cost_estimate=cost(10 * t * rows * query_columns, 8 * t * query_columns, t * rows * QUERY_HEADS),
        name="attend_back",
    )(rank, qkv, kv, kv, grad, cos, sin)


def experts_kernel(
    chunk_ref, h_ref, z_ref, gn_ref, gf_ref, un_ref, uf_ref, wd_ref,
    a_ref, dg_ref, du_ref, eo_ref, dh_ref, weights, eo_acc, dh_acc, dgate_acc, sems,
):
    per, fc, d = weights.shape[2:]
    ct = per * fc

    def copies(side):
        moves = [
            pltpu.make_async_copy((gn_ref, gf_ref)[side], weights.at[side, 0], sems.at[side, 0]),
            pltpu.make_async_copy((un_ref, uf_ref)[side], weights.at[side, 1], sems.at[side, 1]),
        ]
        for k in range(per):
            moves.append(
                pltpu.make_async_copy(
                    wd_ref.at[chunk_ref[side * per + k]], weights.at[side, 2, k], sems.at[side, 2 + k]
                )
            )
        return moves

    for side in range(2):
        for move in copies(side):
            move.start()
    t = z_ref.shape[0]
    gates_high = h_ref[t:, :t]
    gates_low = h_ref[t:, t : 2 * t]
    for side in range(2):
        moves = copies(side)
        slot_row = lax.broadcasted_iota(jnp.int32, (EXTRA, ct), 0)
        slot_col = lax.broadcasted_iota(jnp.int32, (EXTRA, ct), 1) + side * ct
        low = slot_row * fc
        pick = jnp.where((slot_col >= low) & (slot_col < low + fc), 1.0, 0.0).astype(bf16)
        wide = dot_tn(gates_high, pick) + dot_tn(gates_low, pick)
        moves[0].wait()
        wg = weights[side, 0].reshape(ct, d)
        g = dot_nt(h_ref[:t], wg)
        moves[1].wait()
        wu = weights[side, 1].reshape(ct, d)
        u = dot_nt(h_ref[:t], wu)
        for move in moves[2:]:
            move.wait()
        wd = weights[side, 2].reshape(ct, d)
        e = dot_nt(z_ref[...], wd)
        sig = 1.0 / (1.0 + jnp.exp(-g))
        swish = g * sig
        a = swish * u
        da = e * wide
        at = slice(side * ct, (side + 1) * ct)
        ab = (a * wide).astype(bf16)
        dg = (da * u * (sig * (1.0 + g * (1.0 - sig)))).astype(bf16)
        du = (da * swish).astype(bf16)
        a_ref[:, at] = ab
        dg_ref[:, at] = dg
        du_ref[:, at] = du
        dgate = dot_nt(pick, (a * e).astype(bf16))
        if side == 0:
            dgate_acc[...] = dgate
            dh_acc[...] = dot_nn(dg, wg)
            dh_acc[...] += dot_nn(du, wu)
            eo_acc[...] = dot_nn(ab, wd)
        else:
            dgate = dgate_acc[...] + dgate
            high = dgate.astype(dh_ref.dtype)
            dh_ref[t:] = jnp.zeros((EXTRA, d), dh_ref.dtype)
            dh_ref[t:, :t] = high
            dh_ref[t:, t : 2 * t] = (dgate - high.astype(f32)).astype(dh_ref.dtype)
            dh_acc[...] += dot_nn(dg, wg)
            dh_ref[:t] = (dh_acc[...] + dot_nn(du, wu)).astype(dh_ref.dtype)
            eo_ref[...] = (eo_acc[...] + dot_nn(ab, wd)).astype(eo_ref.dtype)


def experts(chunk_of, h, z, wg, wu, wd, sent_type):
    t, d = z.shape
    per, fc = wg[0].shape[0], wg[0].shape[1]
    width = 2 * per * fc
    vmem, hbm = pl.BlockSpec(memory_space=pltpu.VMEM), pl.BlockSpec(memory_space=pl.ANY)
    return pl.pallas_call(
        experts_kernel,
        in_specs=[pl.BlockSpec(memory_space=pltpu.SMEM)] + [vmem] * 2 + [hbm] * 5,
        out_specs=[vmem] * 5,
        out_shape=[
            jax.ShapeDtypeStruct((t, width), bf16),
            jax.ShapeDtypeStruct((t, width), bf16),
            jax.ShapeDtypeStruct((t, width), bf16),
            jax.ShapeDtypeStruct((t, d), sent_type),
            jax.ShapeDtypeStruct((t + EXTRA, d), sent_type),
        ],
        scratch_shapes=[
            pltpu.VMEM((2, 3, per, fc, d), bf16),
            pltpu.VMEM((t, d), f32),
            pltpu.VMEM((t, d), f32),
            pltpu.VMEM((EXTRA, t), f32),
            pltpu.SemaphoreType.DMA((2, 2 + per)),
        ],
        compiler_params=params(48),
        cost_estimate=cost(12 * t * d * width, 6 * d * width),
        name="experts",
    )(chunk_of, h, z, *wg, *wu, wd)


def expert_grads_kernel(n, fc, pairs, *refs):
    out_ref = refs[-1]
    per = out_ref.shape[0]
    rights = refs[pairs * n : -1]
    for which in range(pairs):
        left, right = refs[which * n : (which + 1) * n], rights
        total = dot_tn(left[0][...], right[0][...])
        for s in range(1, n):
            total += dot_tn(left[s][...], right[s][...])
        out_ref[:, which] = total.astype(bf16).reshape(per, fc, total.shape[-1])


def expert_grads(side, fc, lefts, right):
    n = len(right)
    t, width = lefts[0][0].shape
    width = width // 2
    d = right[0].shape[1]
    ct = min(width, 384)
    per = ct // fc
    steps = width // ct
    tile = pl.BlockSpec((t, ct), lambda j: (0, side * steps + j))
    rows = pl.BlockSpec((t, d), lambda j: (0, 0))
    if width % HEAD_WIDTH:
        lefts = [[x[:, side * width : (side + 1) * width] for x in xs] for xs in lefts]
        tile = pl.BlockSpec((t, width), lambda j: (0, 0))
    pairs = len(lefts)
    flat = [x for xs in lefts for x in xs]
    return pl.pallas_call(
        functools.partial(expert_grads_kernel, n, fc, pairs),
        grid=(steps,),
        in_specs=[tile] * (pairs * n) + [rows] * n,
        out_specs=pl.BlockSpec((per, pairs, fc, d), lambda j: (j, 0, 0, 0)),
        out_shape=jax.ShapeDtypeStruct((width // fc, pairs, fc, d), bf16),
        compiler_params=params(58),
        cost_estimate=cost(2 * pairs * n * t * d * width, 2 * pairs * d * width),
        name="expert_grads",
    )(*flat, *right)


def join_kernel(half, slot_ref, *refs):
    out_ref = refs[-1]
    near = slot_ref[pl.program_id(0)] < half

    def run(side):
        at = 0
        for k in range(side, len(refs) - 1, 2):
            block = refs[k][0]
            rows = block.shape[0]
            if out_ref.ndim == 4:
                out_ref[at : at + rows, 0] = block.astype(out_ref.dtype)
            else:
                out_ref[0, at : at + rows] = block.astype(out_ref.dtype)
            at += rows

    pl.when(near)(lambda: run(0))
    pl.when(jnp.logical_not(near))(lambda: run(1))


def join(slot_of, parts, dtype, spread_out=False):
    half = parts[0][0].shape[0]
    m = 2 * half
    tail = parts[0][0].shape[2:]
    rows = sum(near.shape[1] for near, far in parts)
    zeros = (0,) * len(tail)
    specs, flat = [], []
    for pair in parts:
        for x in pair:
            specs.append(pl.BlockSpec((1,) + x.shape[1:], lambda j, s: (s[j] % half, 0) + zeros))
            flat.append(x)
    if spread_out:
        out_spec = pl.BlockSpec((rows, 1) + tail, lambda j, s: (0, j) + zeros)
        shape = (rows, m) + tail
    else:
        out_spec = pl.BlockSpec((1, rows) + tail, lambda j, s: (j, 0) + zeros)
        shape = (m, rows) + tail
    return pl.pallas_call(
        functools.partial(join_kernel, half),
        grid_spec=pltpu.PrefetchScalarGridSpec(
            num_scalar_prefetch=1, grid=(m,), in_specs=specs, out_specs=out_spec
        ),
        out_shape=jax.ShapeDtypeStruct(shape, dtype),
        compiler_params=params(24),
        cost_estimate=cost(0, 6 * math.prod(shape)),
        name="join",
    )(slot_of, *flat)


def columns_kernel(half, counts, slot_ref, near_ref, far_ref, *out_refs):
    j = pl.program_id(0)
    near = slot_ref[j] < half
    at = 0
    for count, out_ref in zip(counts, out_refs):
        mine = (j >= at) & (j < at + count)

        @pl.when(mine & near)
        def _(out_ref=out_ref):
            out_ref[...] = near_ref[0].astype(f32)

        @pl.when(mine & jnp.logical_not(near))
        def _(out_ref=out_ref):
            out_ref[...] = far_ref[0].astype(f32)

        at += count


def columns(slot_of, near, far, widths):
    half, rows, cw = near.shape
    counts = [w // cw for w in widths]
    specs, at = [], 0
    for count in counts:
        specs.append(
            pl.BlockSpec((rows, cw), lambda j, s, at=at, top=count - 1: (0, jnp.clip(j - at, 0, top)))
        )
        at += count
    in_spec = pl.BlockSpec((1, rows, cw), lambda j, s: (s[j] % half, 0, 0))
    return pl.pallas_call(
        functools.partial(columns_kernel, half, counts),
        grid_spec=pltpu.PrefetchScalarGridSpec(
            num_scalar_prefetch=1, grid=(2 * half,), in_specs=[in_spec] * 2, out_specs=specs
        ),
        out_shape=[jax.ShapeDtypeStruct((rows, w), f32) for w in widths],
        compiler_params=params(16),
        cost_estimate=cost(0, 12 * near.size),
        name="columns",
    )(slot_of, near, far)


def arrange_kernel(n, fc, rank_ref, *refs):
    slots, (gate_ref, up_ref) = refs[:n], refs[n:]
    dl = slots[0].shape[1]

    def run(rank):
        for q in range(n):
            block = slots[q ^ rank]
            gate_ref[:, q * dl : (q + 1) * dl] = block[:fc]
            up_ref[:, q * dl : (q + 1) * dl] = block[fc : 2 * fc]

    for rank in range(n):
        pl.when(rank_ref[0] == rank)(functools.partial(run, rank))


def arrange(rank, slots, fc):
    n, d = len(slots), len(slots) * slots[0].shape[1]
    vmem = pl.BlockSpec(memory_space=pltpu.VMEM)
    return pl.pallas_call(
        functools.partial(arrange_kernel, n, fc),
        in_specs=[pl.BlockSpec(memory_space=pltpu.SMEM)] + [vmem] * n,
        out_specs=[vmem] * 2,
        out_shape=[jax.ShapeDtypeStruct((fc, d), bf16)] * 2,
        compiler_params=params(16),
        cost_estimate=cost(0, 8 * fc * d),
        name="arrange",
    )(rank, *slots)


def turn_back_kernel(n, fc, rank_ref, *refs):
    slots, out_ref, rows = refs[:n], refs[n], refs[n + 1]

    def run(rank):
        for k in range(2):
            for q in range(n):
                rows[k, q * fc : (q + 1) * fc] = slots[q ^ rank][k * fc : (k + 1) * fc].astype(f32)

    for rank in range(n):
        pl.when(rank_ref[0] == rank)(functools.partial(run, rank))
    for k in range(2):
        out_ref[k] = rows[k].T.astype(bf16)


def turn_back(rank, slots, fc):
    n, dl = len(slots), slots[0].shape[1]
    if fc % 16 or dl % HEAD_WIDTH or n * fc % HEAD_WIDTH:
        stacked = jnp.stack(slots).reshape(n, 2, fc, dl)
        stacked = jnp.take(stacked, jnp.arange(n) ^ rank, axis=0)
        return jnp.transpose(stacked, (1, 3, 0, 2)).reshape(2, dl, n * fc)
    vmem = pl.BlockSpec(memory_space=pltpu.VMEM)
    return pl.pallas_call(
        functools.partial(turn_back_kernel, n, fc),
        in_specs=[pl.BlockSpec(memory_space=pltpu.SMEM)] + [vmem] * n,
        out_specs=vmem,
        out_shape=jax.ShapeDtypeStruct((2, dl, n * fc), bf16),
        scratch_shapes=[pltpu.VMEM((2, n * fc, dl), f32)],
        compiler_params=params(24),
        cost_estimate=cost(0, 8 * n * fc * dl),
        name="turn_back",
    )(rank, *slots)


class Rounds:
    def __init__(self):
        self.gate, self.made, self.later = (), [], []

    def enter(self, x):
        return after(x, *self.gate) if self.gate else x

    def leave(self, *xs):
        self.made.extend(xs)
        return xs[0]

    def leave_late(self, *xs):
        self.later.extend(xs)
        return xs[0]

    def turn(self):
        self.gate, self.made, self.later = tuple(self.made), self.later, []


class Along:
    def __init__(self, rounds):
        self.rounds = rounds
        self.n, self.m = lax.axis_size("cp"), lax.axis_size("dp")
        self.r, self.i = lax.axis_index("cp"), lax.axis_index("dp")
        self.bits = self.m.bit_length() - 1
        assert 1 << self.bits == self.m and self.bits > 1
        self.inner = self.bits - 1
        slots = jnp.arange(self.m, dtype=jnp.int32)
        self.chunk_of = self.i ^ (((slots & (self.m // 2 - 1)) << 1) | (slots >> self.inner))
        offset = slots ^ self.i
        self.slot_of = (offset >> 1) | ((offset & 1) << self.inner)

    def send(self, x, axis, pairs, late=False):
        leave = self.rounds.leave_late if late else self.rounds.leave
        return leave(lax.ppermute(self.rounds.enter(x), axis, pairs))

    def swap(self, x, bit, late=False):
        mask = 1 if bit == self.inner else 2 << bit
        return self.send(x, "dp", [(k, k ^ mask) for k in range(self.m)], late)

    def cross(self, x, s, keep=None, late=False):
        pairs = [(k, k ^ s) for k in range(self.n)]
        return self.send(x, "cp", [p for p in pairs if keep is None or keep(*p)], late)

    def orders(self):
        up = list(range(self.inner))
        return up, up[::-1]

    def pieces(self, x, s):
        return lax.dynamic_index_in_dim(x, self.r ^ s, 0, keepdims=False)

    def scatter_cp(self, x):
        return [self.pieces(x, 0)] + [self.cross(self.pieces(x, s), s) for s in range(1, self.n)]

    def ranked(self, slots):
        for bit in range(self.n.bit_length() - 1):
            turned = (self.r >> bit & 1) == 1
            slots = [jnp.where(turned, slots[k ^ 1 << bit], slots[k]) for k in range(self.n)]
        return jnp.stack(slots)

    def gather_cp(self, x):
        return [x] + [self.cross(x, s) for s in range(1, self.n)]


class Gather:
    def __init__(self, along, *xs):
        self.along, self.parts, self.at = along, [{0: x} for x in xs], 0

    def step(self, late=False):
        for k, held in enumerate(self.parts):
            bit = self.along.orders()[k % 2][self.at]
            slots = sorted(held)
            got = self.along.swap(jnp.stack([held[h] for h in slots]), bit, late)
            for p, h in enumerate(slots):
                held[h | 1 << bit] = got[p]
        self.at += 1

    def rest(self, late=False):
        while self.at < self.along.inner:
            self.step(late)

    def finish(self, late=False):
        self.rest(late)
        near = [jnp.stack([held[h] for h in sorted(held)]) for held in self.parts]
        return [(x, self.along.swap(x, self.along.inner, late)) for x in near]


class Reduce:
    def __init__(self, along, far):
        self.along, self.at = along, 0
        self.got = along.swap(far, along.inner)

    def add(self, near):
        cut = near.shape[1] // 2
        self.parts = [
            {h: near[h, at].astype(f32) + self.got[h, at].astype(f32) for h in range(self.along.m // 2)}
            for at in (slice(0, cut), slice(cut, None))
        ]

    def step(self, late=False):
        for k, held in enumerate(self.parts):
            bit = self.along.orders()[1 - k][self.at]
            sent = jnp.stack([held[h].astype(bf16) for h in sorted(held) if h >> bit & 1])
            more = self.along.swap(sent, bit, late)
            kept = [h for h in sorted(held) if not h >> bit & 1]
            self.parts[k] = {h: held[h] + more[p].astype(f32) for p, h in enumerate(kept)}
        self.at += 1

    def rest(self, late=False):
        while self.at < self.along.inner:
            self.step(late)

    def finish(self):
        self.rest()
        return jnp.concatenate([p[0] for p in self.parts], 0).astype(bf16)


class Relay:
    inside, outside, turned = [(1, 2), (2, 1)], [(1, 0), (2, 3)], [(0, 1), (3, 2)]

    def __init__(self, along, x):
        self.along, self.x, self.four = along, x, along.n == 4

    def one(self):
        self.first = self.along.cross(self.x, 1)

    def middle(self):
        if self.four:
            self.third = self.along.send(self.x, "cp", self.inside)

    def two(self, late=False):
        self.second = self.along.cross(self.x, 2, late=late)

    def ends(self):
        along = self.along
        if self.four:
            outer = along.send(self.second, "cp", self.outside)
            self.third = [jnp.where((along.r == 1) | (along.r == 2), self.third, outer)]
        else:
            self.third = [along.cross(self.x, s) for s in range(3, along.n)]

    def slots(self):
        return [self.x, self.first, self.second, *self.third]


def norm_forward(values, gain_vec):
    inverse = lax.rsqrt(jnp.mean(values * values, -1, keepdims=True) + norm_eps)
    scaled = values * inverse
    return (scaled * gain_vec, scaled, inverse)


def norm_backward(gradient, gain_vec, scaled, inverse):
    gain_grad = jnp.sum(gradient * scaled, 0)
    inner_vals = gradient * gain_vec
    return (
        inverse * (inner_vals - scaled * jnp.mean(inner_vals * scaled, -1, keepdims=True)),
        gain_grad,
    )


def rotary(positions):
    half = HEAD_WIDTH // 2
    frequency = rope_base ** (-2.0 * jnp.arange(half, dtype=f32) / HEAD_WIDTH)
    angles = positions.astype(f32)[:, None] * frequency[None, :]
    cos, sin = jnp.cos(angles), jnp.sin(angles)
    return jnp.concatenate([cos, cos], 1), jnp.concatenate([-sin, sin], 1)


def local(
    tokens, routes, out_grad, norm_attn, w_query, key_weight, value_weight, w_out,
    norm_mix, w_router, w_gate, w_up, w_down,
):
    rounds = Rounds()
    along = Along(rounds)
    n, m, r, i = along.n, along.m, along.r, along.i
    t, d = tokens.shape[1], tokens.shape[2]
    assert t == BLK
    dl, ff, fs = w_query.shape[0], w_gate.shape[2], w_down.shape[1]
    sub = m // EXPERTS
    fc = fs // sub
    rc = dl // m
    inputs = tokens[0].astype(f32)
    route_rows = routes[0]
    dz = out_grad[0]
    up = lambda a, b: b > a
    down = lambda a, b: b < a

    w_qkv = jnp.concatenate([w_query, key_weight, value_weight], 1)
    cw = w_qkv.shape[1] // m
    small = jnp.concatenate([norm_attn[None], norm_mix[None], w_router.T], 0).reshape(-1)
    tail = -(-small.shape[0] // (16 * cw)) * 16
    small = jnp.concatenate([small, jnp.zeros((tail * cw - small.shape[0],), bf16)]).reshape(tail, cw)
    sent = jnp.concatenate([lax.dynamic_slice_in_dim(w_qkv, i * cw, cw, 1), small], 0)
    got = along.ranked(along.gather_cp(sent))
    own_qkv = got[:, :dl].reshape(d, cw)
    small = got[:, dl:].reshape(n, tail * cw)[:, : (2 + EXPERTS) * dl].reshape(n, 2 + EXPERTS, dl)
    small = jnp.swapaxes(small, 0, 1).reshape(2 + EXPERTS, d)
    gain_one, gain_two = small[0].astype(f32), small[1].astype(f32)
    router = small[2:]
    flipped = [
        lax.dynamic_index_in_dim(w, i // sub, 0, keepdims=False).T.reshape(n, sub, fc, dl)
        for w in (w_gate, w_up)
    ]
    flipped = lax.dynamic_index_in_dim(jnp.stack(flipped, 1), i % sub, 2, keepdims=False).reshape(n, 2 * fc, dl)
    flipped = rounds.leave(flipped)
    out_rows = lax.dynamic_slice_in_dim(w_out, i * rc, rc, 0)
    cos, sin = rotary(r * t + jnp.arange(t, dtype=jnp.int32))
    rounds.leave(cos, sin)

    rounds.turn()
    qkv_gather = Gather(along, own_qkv[: d // 2], own_qkv[d // 2 :])
    qkv_gather.step()
    own_out = along.gather_cp(out_rows)
    normed_one, scaled_one, inverse_one = norm_forward(inputs, gain_one)
    h1 = rounds.leave(normed_one.astype(bf16))
    rounds.turn()
    qkv_gather.rest()
    mix = [along.pieces(flipped, 0)] + [along.cross(along.pieces(flipped, s), s) for s in (1, 2)]
    own_out = rounds.leave(along.ranked(own_out))
    rounds.turn()
    qkv_a, qkv_b = qkv_gather.finish()
    mix.extend(along.cross(along.pieces(flipped, s), s, late=True) for s in range(3, n))
    rounds.turn()
    rank = r.reshape(1)
    out_gather = Gather(along, own_out[: n // 2], own_out[n // 2 :])
    out_gather.step()
    qkv = rounds.leave(project(along.slot_of, rounds.enter(h1), qkv_a, qkv_b, cos, sin))
    rounds.turn()

    own_kv = qkv[:, query_columns:]
    kv = jnp.concatenate([own_kv] + [along.cross(own_kv, s, up) for s in range(1, n)], 0)
    out_gather.rest()
    if dl % HEAD_WIDTH == 0:
        gate_rows, up_rows = arrange(rank, [rounds.enter(x) for x in mix], fc)
    else:
        gate_rows, up_rows = jnp.swapaxes(along.ranked(mix), 0, 1).reshape(2, fc, d)
    mix_gather = Gather(along, gate_rows, up_rows)
    mix_gather.step()
    rounds.turn()
    z_relay = Relay(along, dz)
    z_relay.two()
    mix_gather.rest()
    out_a, out_b = out_gather.finish()
    ob = rounds.leave(attend(rank, qkv, rounds.enter(kv)))
    full_out = join(along.slot_of, [out_a, out_b], bf16, True).reshape(n * dl, d)
    full_out = rounds.leave(full_out)
    rounds.turn()
    z_relay.one()
    z_relay.middle()
    wg, wu = mix_gather.finish()
    wd = w_down.reshape(m, fc, d)

    middle = inputs + dot_nn(rounds.enter(ob), full_out)
    normed_two, scaled_two, inverse_two = norm_forward(middle, gain_two)
    h2 = normed_two.astype(bf16)
    logits = dot_nt(h2, router)
    experts_range = jnp.arange(EXPERTS, dtype=jnp.int32)
    route_flags = (route_rows[:, :, None] == experts_range).astype(f32)
    chosen = jnp.sum(logits[:, None, :] * route_flags, -1)
    raised = jnp.exp(chosen - jnp.max(chosen, -1, keepdims=True))
    gate_vals = raised / jnp.sum(raised, -1, keepdims=True)
    slot_flags = (route_rows[:, :, None] == along.chunk_of // sub).astype(f32)
    gates = jnp.sum(gate_vals[:, :, None] * slot_flags, 1).T
    gates = jnp.concatenate([gates, jnp.zeros((EXTRA - m, t), f32)], 0)
    gates_high = gates.astype(bf16)
    gates_low = (gates - gates_high.astype(f32)).astype(bf16)
    gates = jnp.concatenate([gates_high, gates_low, jnp.zeros((EXTRA, d - 2 * t), bf16)], 1)
    h_sent = rounds.leave(jnp.concatenate([h2, gates], 0))
    rounds.turn()

    h_relay = Relay(along, h_sent)
    h_relay.one()
    h_relay.middle()

    def run(h, z, sent_type=bf16):
        results = experts(along.chunk_of, rounds.enter(h), z, wg, wu, wd, sent_type)
        rounds.leave(*results)
        return results

    done = [run(h_sent, dz, f32)]
    rounds.turn()
    h_relay.two()
    z_relay.ends()
    done.append(run(h_relay.first, z_relay.first))
    rounds.turn()
    h_relay.ends()
    done.append(run(h_relay.second, z_relay.second))
    rounds.turn()
    h_slots, z_slots = h_relay.slots(), z_relay.slots()
    h2_back = done[0][4] + along.cross(done[1][4], 1).astype(f32)
    done.extend(run(h_slots[s], z_slots[s]) for s in range(3, n))
    rounds.turn()
    triples = [[rounds.enter(x[k]) for x in done] for k in range(3)]
    second = done[2][4]
    if n == 4:
        h2_back = h2_back + along.send(done[3][4], "cp", Relay.inside).astype(f32)
        second = (second.astype(f32) + along.send(done[3][4], "cp", Relay.turned).astype(f32)).astype(bf16)
    else:
        for s in range(3, n):
            h2_back = h2_back + along.cross(done[s][4], s).astype(f32)
    mix_far = rounds.leave(expert_grads(1, fc, triples[1:], h_slots).reshape(m // 2, 2 * fc, d))
    mix_reduce = Reduce(along, mix_far)
    mix_near = rounds.leave(expert_grads(0, fc, triples[1:], h_slots).reshape(m // 2, 2 * fc, d))
    rounds.turn()
    h2_back = h2_back + along.cross(second, 2).astype(f32)
    mix_reduce.add(mix_near)
    mix_reduce.rest()
    acts = [rounds.enter(x) for x in triples[0]]
    down_grads = [expert_grads(side, fc, [acts], z_slots).reshape(m // 2, fc, d) for side in (0, 1)]
    down_grads = rounds.leave(join(along.slot_of, [down_grads], bf16))
    rounds.turn()
    own_mix = mix_reduce.finish()
    back = [lax.dynamic_slice_in_dim(own_mix, (r ^ s) * dl, dl, 1) for s in range(n)]
    back = [back[0]] + [along.cross(back[s], s) for s in range(1, n)]
    mixed = done[0][3] + along.cross(done[1][3], 1).astype(f32)
    h2_back = rounds.enter(h2_back)
    slot_gate_grad = h2_back[t : t + m, :t] + h2_back[t : t + m, t : 2 * t]
    gate_grad = jnp.sum(slot_gate_grad.T[:, None, :] * slot_flags, -1)
    weighted = gate_vals * gate_grad
    chosen_grad = weighted - gate_vals * jnp.sum(weighted, -1, keepdims=True)
    logit_grad = jnp.sum(chosen_grad[:, :, None] * route_flags, 1).astype(bf16)
    router_grad = dot_tn(logit_grad, h2)
    h2_grad = h2_back[:t] + dot_nn(logit_grad, router)
    middle_norm_grad, gain_two_grad = norm_backward(h2_grad, gain_two, scaled_two, inverse_two)
    middle_grad = dz.astype(f32) + middle_norm_grad
    branch = middle_grad.astype(bf16)

    dob = dot_nt(branch, full_out).astype(bf16)
    dq, dkv = attend_back(rank, qkv, kv, dob, cos, sin)
    rounds.leave(dkv)
    rounds.turn()
    out_grads = jnp.swapaxes(dot_tn(ob, rounds.enter(branch)).astype(bf16).reshape(n, m, rc, d), 0, 1).reshape(m * n * rc, d)
    out_grads = lax.psum_scatter(out_grads, "dp", scatter_dimension=0, tiled=True)
    dkv_own = dkv[:, :t].astype(f32)
    for s in range(1, n):
        dkv_own = dkv_own + along.cross(dkv[:, s * t : (s + 1) * t], s, down).astype(f32)
    back = turn_back(rank, [rounds.enter(x) for x in back], fc)
    back_gather = Gather(along, back[0], back[1])
    back_gather.step()
    rounds.turn()
    back_gather.rest()
    down_grads = lax.psum(rounds.enter(after(down_grads, out_grads)), "dp")
    grad_w_down = down_grads.reshape(EXPERTS, fs, d).astype(f32)
    second_out = done[2][3]
    if n == 4:
        mixed = mixed + along.send(done[3][3], "cp", Relay.inside).astype(f32)
        second_out = second_out.astype(f32) + along.send(done[3][3], "cp", Relay.turned).astype(f32)
        second_out = second_out.astype(bf16)
    dkv_own = rounds.enter(dkv_own)
    dk = dkv_own[0].reshape(t, KEY_VALUE_HEADS, HEAD_WIDTH)
    half = HEAD_WIDTH // 2
    dk = dk * cos[:, None] - jnp.concatenate([dk[..., half:], dk[..., :half]], -1) * sin[:, None]
    dqkv = jnp.concatenate([dq, dk.reshape(t, key_columns).astype(bf16), dkv_own[1].astype(bf16)], 1)
    h1_grad, qkv_near, qkv_far = project_back(along.chunk_of, h1, dqkv, qkv_a, qkv_b)
    rounds.leave(h1_grad, qkv_near, qkv_far)
    qkv_reduce = Reduce(along, qkv_far)
    rounds.turn()
    qkv_reduce.add(qkv_near)
    qkv_reduce.step()
    back_slots = back_gather.finish()
    out_grads = lax.all_to_all(rounds.enter(out_grads.reshape(n, rc, d)), "cp", 0, 0, tiled=True)
    out_grads = rounds.leave(jnp.sum(out_grads.astype(f32), 0).astype(bf16))
    input_norm_grad, gain_one_grad = norm_backward(rounds.enter(h1_grad), gain_one, scaled_one, inverse_one)
    input_grad = (middle_grad + input_norm_grad).astype(bf16)[None]
    small_grads = jnp.concatenate([gain_one_grad[None], gain_two_grad[None], router_grad], 0)
    rounds.leave(small_grads)
    rounds.turn()
    qkv_reduce.rest()
    small_grads = small_grads + along.swap(small_grads, along.inner)
    second_out = rounds.enter(second_out)
    mixed = mixed + lax.ppermute(second_out, "cp", [(k, k ^ 2) for k in range(n)]).astype(f32)
    grad_w_out = lax.all_gather(rounds.enter(out_grads), "dp", axis=0, tiled=True).astype(f32)
    grads = []
    for slots in back_slots:
        g = rounds.leave(join(along.slot_of, [[rounds.enter(x) for x in slots]], f32))
        if sub > 1:
            g = g.reshape(EXPERTS, sub, dl, n, fc)
            g = jnp.transpose(g, (0, 2, 3, 1, 4))
        grads.append(g.reshape(EXPERTS, dl, ff))
    grad_w_gate, grad_w_up = grads
    rounds.turn()
    own_qkv = qkv_reduce.finish().reshape(n, dl, cw)
    own_qkv = [along.pieces(own_qkv, 0)] + [along.cross(along.pieces(own_qkv, s), s) for s in range(1, n)]
    own_qkv = functools.reduce(jnp.add, [x.astype(f32) for x in own_qkv]).astype(bf16)
    small_grads = small_grads + along.swap(small_grads, 0)
    if n != 4:
        for s in range(3, n):
            mixed = mixed + along.cross(done[s][3], s).astype(f32)
    rounds.turn()
    qkv_gather = Gather(along, own_qkv)
    qkv_gather.step()
    for bit in range(1, along.inner):
        small_grads = small_grads + along.swap(small_grads, bit)
    rounds.turn()
    qkv_gather.rest()
    small_grads = small_grads + along.cross(small_grads, 1)
    rounds.turn()
    (qkv_slots,) = qkv_gather.finish()
    for bit in range(1, n.bit_length() - 1):
        small_grads = small_grads + along.cross(small_grads, 1 << bit)
    output = (middle + mixed).astype(bf16)[None]
    small_grads = lax.dynamic_index_in_dim(small_grads.reshape(2 + EXPERTS, n, dl), r, 1, keepdims=False)
    grad_w_query, grad_w_key, grad_w_value = columns(
        along.slot_of, *qkv_slots, (query_columns, key_columns, key_columns)
    )
    return (
        output,
        input_grad,
        small_grads[0],
        grad_w_query,
        grad_w_key,
        grad_w_value,
        grad_w_out,
        small_grads[1],
        small_grads[2:].T,
        grad_w_gate,
        grad_w_up,
        grad_w_down,
    )


def solution(mesh):
    seq = P("dp", "cp", None)
    row, mid = P("cp", None), P(None, "cp", None)
    in_specs = (seq, seq, seq, P("cp"), row, row, row, row, P("cp"), row, mid, mid, mid)
    out_specs = (seq, seq, P("cp"), row, row, row, row, P("cp"), row, mid, mid, mid)
    return jax.shard_map(local, mesh=mesh, in_specs=in_specs, out_specs=out_specs, check_vma=False)
```
